128 devices in a mesh: energy: 16 (over y, z_lo, core), momentum: 8 (over z_hi, x).
Axes of the slice: x: 4, y: 4, z: 4 (z_hi: 2, z_lo: 2; z = z_hi * 2 + z_lo), core: 2. Of those that a mesh axis runs over, the one named last changes fastest.
Arguments:
- green_blocks: float32 [2, 16, 8, 200, 1024], P(None, 'energy', 'momentum'), may hold values from -6 to 6
- couple_matrix: float32 [3, 100, 1024], P(None, None, ('energy', 'momentum')), may hold values from -1.8 to 1.8
- occupation: float32 [3], replicated, may hold values from 0.1 to 3
- energy_shift: int32 [3], replicated, may hold values from 1 to 15, as said below
- branch_weight: float32 [8, 3], replicated, may hold values from 0.3 to 3
- pair_branch: int32 [8, 8], replicated, may hold values from 0 to 7
Outputs:
- self_energy: float32 [2, 16, 8, 200, 1024], P(None, 'energy', 'momentum')
The draws below stay inside these ranges and needn't reach their ends.
Inputs may be any that keep to these rules, and one draw needn't show every extreme that they name: `energy_shift`: the branches' shifts are distinct.
All inputs are finite; a program needn't handle non-finite values.
Results may differ from the reference program's by a relative error of at most 0.0001.
Values sent between devices are 32-bit elements; how exact they have to be, the bound alone decides.
No kernel may reach another device: no remote copies, remote signals or barrier semaphores. Data moves between devices by JAX's collectives and lax.ppermute only.
A program may use at most 192 MiB of HBM per device.

```python
import math
import jax
import jax.numpy as jnp
from jax import lax

ORB = 10
MODES = 3
NE = 16
NK = 8
ATOMS = 1024
NQ = 8


def draw_energy_shift(key, part):
    key = jax.random.fold_in(key, 11)
    first_key, second_key = jax.random.split(key)
    middle = jax.random.permutation(first_key, NE - 3)[:MODES - 2].astype(jnp.int32) + 2
    values = jnp.concatenate([jnp.array([1, NE - 1], dtype=jnp.int32), middle])
    order = jax.random.permutation(second_key, MODES)
    return values[order].astype(jnp.int32)


def place_ends(result, stream_key, low, top_value):
    extent = result.shape
    place = [jax.random.randint(jax.random.fold_in(stream_key, axis), (), 0, extent[axis]) for axis in range(len(extent))]
    result = result.at[tuple(place)].set(low)
    longest = extent.index(max(extent))
    place[longest] = (place[longest] + 1) % extent[longest]
    return result.at[tuple(place)].set(top_value)


def levels(stream_key, shape, shards, low, high):
    factor_of = 1.0
    for position, shards_of in shards:
        steps = jax.random.uniform(jax.random.fold_in(jax.random.fold_in(stream_key, 6), position), (shards_of,), jnp.float32, low / len(shards), high / len(shards))
        factor_of = factor_of * jnp.repeat(jnp.exp(steps), shape[position] // shards_of).reshape((-1,) + (1,) * (len(shape) - 1 - position))
    return factor_of


def bell_draw(rng, dims, deviation, limit, cuts=(), held_as=jnp.bfloat16):
    drawn = jax.random.normal(rng, dims, jnp.float32) * deviation
    if len(cuts) > 0:
        drawn = levels(rng, dims, cuts, -0.22, 0.18) * drawn
    return jnp.clip(drawn, min=-limit, max=limit).astype(held_as)


def setup_inputs(seed: int = 0) -> dict:
    keys = jax.random.split(jax.random.key(seed), 7)
    green_blocks = bell_draw(keys[0], (2, NE, NK, 2 * ORB * ORB, ATOMS), 1.0, 6.0, ((1, 16), (2, 8)), jnp.float32)
    couple_matrix = bell_draw(keys[1], (MODES, ORB * ORB, ATOMS), 0.3, 1.8, ((2, 128),), jnp.float32)
    occupation = jnp.clip(jnp.exp(jax.random.uniform(keys[2], (MODES,), jnp.float32, math.log(0.1), math.log(3.0))), 0.1, 3.0)
    energy_shift = draw_energy_shift(jax.random.fold_in(keys[6], 71), 0)
    branch_weight = jnp.clip(jnp.exp(jax.random.uniform(keys[4], (NQ, MODES), jnp.float32, math.log(0.3), math.log(3.0))), 0.3, 3.0)
    pair_branch = place_ends(jax.random.randint(keys[5], (NK, NK), 0, NQ), jax.random.fold_in(keys[5], 1), 0, NQ - 1).astype(jnp.int32)
    return dict(green_blocks=green_blocks, couple_matrix=couple_matrix, occupation=occupation, energy_shift=energy_shift, branch_weight=branch_weight, pair_branch=pair_branch)


def transform(field, couple, occupation, energy_shift, kind_index):
    energies = field.shape[0]
    momenta = field.shape[1]
    atoms_here = field.shape[3]
    padded = jnp.pad(field, ((energies, energies), (0, 0), (0, 0), (0, 0)))
    results = []
    for mode_index in range(couple.shape[0]):
        upper_part = lax.dynamic_slice_in_dim(padded, energies + energy_shift[mode_index], energies, 0)
        lower_part = lax.dynamic_slice_in_dim(padded, energies - energy_shift[mode_index], energies, 0)
        combined = (occupation[mode_index] + 1.0 - kind_index) * upper_part + (occupation[mode_index] + kind_index) * lower_part
        blocks = combined.reshape(energies, momenta, 2, ORB, ORB, atoms_here)
        coupling = couple[mode_index].reshape(ORB, ORB, atoms_here)
        left_product = jnp.einsum('ija,ekrjla->ekrila', coupling, blocks, precision=lax.Precision.HIGHEST)
        sandwich = jnp.einsum('ekrila,nla->ekrina', left_product, coupling, precision=lax.Precision.HIGHEST)
        results.append(sandwich.reshape(energies, momenta, 2 * ORB * ORB, atoms_here))
    return jnp.stack(results)


def mixing(branch_weight, pair_branch):
    onehot = (pair_branch[:, :, None] == jnp.arange(branch_weight.shape[0], dtype=jnp.int32)).astype(jnp.float32)
    return jnp.einsum('kjq,qm->mkj', onehot, branch_weight, precision=lax.Precision.HIGHEST)


def reference(green_blocks, couple_matrix, occupation, energy_shift, branch_weight, pair_branch):
    mixing_table = mixing(branch_weight, pair_branch) / NK
    results = []
    for kind_index in range(2):
        transformed = transform(green_blocks[kind_index], couple_matrix, occupation, energy_shift, kind_index)
        results.append(jnp.einsum('mkj,mejxa->ekxa', mixing_table, transformed, precision=lax.Precision.HIGHEST))
    return jnp.stack(results)
```

```python
import jax
import jax.numpy as jnp
import numpy as np
from jax import lax
from jax.experimental import pallas as pl
from jax.experimental.pallas import tpu as pltpu
from jax.sharding import PartitionSpec as P

ORB = 10
PAIRS = ORB * ORB
LANES = 128
ATOMS_HERE = 8
ROWS = 25
POINTS = 128
MODES = 3
AXES = ("energy", "momentum")
HIGHEST = lax.Precision.HIGHEST
PARAMS = pltpu.CompilerParams(vmem_limit_bytes=48 * 1024 * 1024)


def split(value):
    high = value.astype(jnp.bfloat16)
    low = (value - high.astype(jnp.float32)).astype(jnp.bfloat16)
    return high, low


def dot(left, right):
    return lax.dot(left, right, preferred_element_type=jnp.float32)


def pack_kernel(green_ref, out_ref, rest_ref):
    for tile in range(3):
        turned = green_ref[LANES * tile : LANES * (tile + 1), :].T
        for owner in range(16):
            out_ref[ROWS * owner + 8 * tile : ROWS * owner + 8 * tile + 8, :] = turned[
                8 * owner : 8 * owner + 8, :
            ]
    rest = green_ref[384:400, :]
    rest_ref[...] = jnp.concatenate([rest, jnp.zeros((112, LANES), jnp.float32)], axis=0).T
    total = rest_ref[pl.ds(0, 16, stride=8), :]
    for atom in range(1, 8):
        total = total + pltpu.roll(rest_ref[pl.ds(atom, 16, stride=8), :], 16 * atom, 1)
    out_ref[pl.ds(24, 16, stride=ROWS), :] = total


def unpack_kernel(in_ref, out_ref, rest_ref):
    for tile in range(3):
        pieces = [
            in_ref[ROWS * owner + 8 * tile : ROWS * owner + 8 * tile + 8, :]
            for owner in range(16)
        ]
        out_ref[LANES * tile : LANES * (tile + 1), :] = jnp.concatenate(pieces, axis=0).T
    rest = in_ref[pl.ds(24, 16, stride=ROWS), :]
    rest_ref[pl.ds(0, 16, stride=8), :] = rest
    for atom in range(1, 8):
        rest_ref[pl.ds(atom, 16, stride=8), :] = pltpu.roll(rest, LANES - 16 * atom, 1)
    out_ref[384:400, :] = rest_ref[...].T[:16, :]


def prepare_kernel(
    occ_ref, shift_ref, couple_ref, mix_ref, cols_ref, rows_ref, out_ref, high_ref, low_ref
):
    spread = lax.dot(
        couple_ref[...], cols_ref[...], precision=HIGHEST, preferred_element_type=jnp.float32
    )
    for index in range(ATOMS_HERE * MODES):
        atom, mode = index // MODES, index % MODES
        part = spread[16 * index : 16 * index + 16, :]
        first = lax.dot(
            rows_ref[:LANES, :], part[:, :LANES], precision=HIGHEST,
            preferred_element_type=jnp.float32,
        )
        second = lax.dot(
            rows_ref[LANES:, :], part[:, LANES:], precision=HIGHEST,
            preferred_element_type=jnp.float32,
        )
        high, low = split(first * second)
        base = 2 * LANES * mode
        out_ref[atom, base : base + LANES, :LANES] = high
        out_ref[atom, base : base + LANES, LANES:] = low
        out_ref[atom, base + LANES : base + 2 * LANES, :LANES] = high
        out_ref[atom, base + LANES : base + 2 * LANES, LANES:] = jnp.zeros_like(low)
    row = lax.broadcasted_iota(jnp.int32, (POINTS, POINTS), 0) >> 3
    col = lax.broadcasted_iota(jnp.int32, (POINTS, POINTS), 1) >> 3
    for mode in range(MODES):
        step = shift_ref[mode]
        above = col == row + step
        below = col == row - step
        mixing = mix_ref[mode]
        for kind in range(2):
            upper = occ_ref[mode] + (1.0 - kind)
            lower = occ_ref[mode] + float(kind)
            moved = jnp.where(above, upper, 0.0) + jnp.where(below, lower, 0.0)
            high, low = split(moved * mixing)
            high_ref[kind, POINTS * mode : POINTS * (mode + 1), :] = high
            low_ref[kind, POINTS * mode : POINTS * (mode + 1), :] = low


def compute_kernel(x_ref, weight_ref, high_ref, low_ref, out_ref):
    lane = lax.broadcasted_iota(jnp.int32, (POINTS, LANES), 1)
    rest = x_ref[pl.ds(24, POINTS, stride=ROWS), :]
    rest_out = jnp.zeros((POINTS, LANES), jnp.float32)
    for atom in range(ATOMS_HERE):
        tiles = [x_ref[pl.ds(8 * t + atom, POINTS, stride=ROWS), :] for t in range(3)]
        tiles.append(pltpu.roll(rest, (LANES - 16 * atom) % LANES, 1) if atom else rest)
        blocks = [tiles[0]]
        for b in range(1, 4):
            joined = jnp.where(lane < PAIRS - 28 * b, tiles[b], tiles[b - 1])
            blocks.append(pltpu.roll(joined, 28 * b, 1))
        rows = []
        for kind in range(2):
            x_high, x_low = split(jnp.concatenate(blocks[2 * kind : 2 * kind + 2], axis=1))
            table = high_ref[kind]
            moved = dot(
                jnp.concatenate([table, table], axis=1), jnp.concatenate([x_high, x_low], axis=0)
            ) + dot(low_ref[kind], x_high)
            y_high, y_low = split(moved)
            for part in range(2):
                lanes = slice(LANES * part, LANES * (part + 1))
                pieces = []
                for mode in range(MODES):
                    points = slice(POINTS * mode, POINTS * (mode + 1))
                    pieces += [y_high[points, lanes], y_low[points, lanes]]
                rows.append(jnp.concatenate(pieces, axis=1))
        result = dot(jnp.concatenate(rows, axis=0), weight_ref[atom])
        result = result[:, :LANES] + result[:, LANES:]
        turned = [result[:POINTS]]
        for b in range(1, 4):
            turned.append(
                pltpu.roll(result[POINTS * b : POINTS * (b + 1)], LANES - 28 * b, 1)
            )
        for t in range(3):
            out_ref[pl.ds(8 * t + atom, POINTS, stride=ROWS), :] = jnp.where(
                lane < PAIRS - 28 * t, turned[t], turned[t + 1]
            )
        tail = jnp.where(lane < 16, turned[3], 0.0)
        rest_out = rest_out + (pltpu.roll(tail, 16 * atom, 1) if atom else tail)
    out_ref[pl.ds(24, POINTS, stride=ROWS), :] = rest_out


def constants():
    pair = np.arange(LANES)
    valid = pair < PAIRS
    cols = np.zeros((LANES, 2 * LANES), np.float32)
    rows = np.zeros((2 * LANES, 16), np.float32)
    for k in range(ORB):
        cols[k, :LANES] = valid & (pair // ORB == k)
        cols[k, LANES:] = valid & (pair % ORB == k)
        rows[:LANES, k] = valid & (pair // ORB == k)
        rows[LANES:, k] = valid & (pair % ORB == k)
    return jnp.asarray(cols), jnp.asarray(rows)


def exchange(message):
    moved = lax.all_to_all(
        message.reshape(POINTS, ROWS, 1, LANES), AXES, split_axis=0, concat_axis=0, tiled=True
    )
    return moved.reshape(POINTS * ROWS, LANES)


def mixing(branch_weight, pair_branch):
    onehot = (
        pair_branch[:, :, None] == jnp.arange(branch_weight.shape[0], dtype=jnp.int32)
    ).astype(jnp.float32)
    return jnp.einsum("kjq,qm->mkj", onehot, branch_weight, precision=HIGHEST)


def on_device(green_blocks, couple_matrix, occupation, energy_shift, branch_weight, pair_branch):
    f32, bf16 = jnp.float32, jnp.bfloat16
    tiles = green_blocks.shape[4] // LANES
    message = pl.pallas_call(
        pack_kernel,
        grid=(tiles,),
        in_specs=[pl.BlockSpec((400, LANES), lambda i: (0, i))],
        out_specs=pl.BlockSpec((400, LANES), lambda i: (i, 0)),
        out_shape=jax.ShapeDtypeStruct((POINTS * ROWS, LANES), f32),
        scratch_shapes=[pltpu.VMEM((LANES, LANES), f32)],
        compiler_params=PARAMS,
        name="pack",
    )(green_blocks.reshape(400, tiles * LANES))
    received = exchange(message)

    table = jnp.tile(mixing(branch_weight, pair_branch) / pair_branch.shape[0], (1, 16, 16))
    turned = couple_matrix.reshape(MODES, ORB, ORB, ATOMS_HERE).transpose(3, 0, 2, 1)
    turned = jnp.pad(turned, ((0, 0), (0, 0), (0, 6), (0, LANES - ORB))).reshape(-1, LANES)
    cols, rows = constants()
    smem = pl.BlockSpec(memory_space=pltpu.SMEM)
    vmem = pl.BlockSpec(memory_space=pltpu.VMEM)
    weight, high, low = pl.pallas_call(
        prepare_kernel,
        in_specs=[smem, smem, vmem, vmem, vmem, vmem],
        out_specs=[vmem, vmem, vmem],
        out_shape=[
            jax.ShapeDtypeStruct((ATOMS_HERE, 2 * MODES * LANES, 2 * LANES), bf16),
            jax.ShapeDtypeStruct((2, MODES * POINTS, POINTS), bf16),
            jax.ShapeDtypeStruct((2, MODES * POINTS, POINTS), bf16),
        ],
        compiler_params=PARAMS,
        cost_estimate=pl.CostEstimate(flops=10**9, bytes_accessed=4 * 10**6, transcendentals=0),
        name="prepare",
    )(occupation, energy_shift, turned, table, cols, rows)

    result = pl.pallas_call(
        compute_kernel,
        in_specs=[vmem] * 4,
        out_specs=vmem,
        out_shape=jax.ShapeDtypeStruct((POINTS * ROWS, LANES), f32),
        compiler_params=PARAMS,
        name="compute",
    )(received, weight, high, low)
    returned = exchange(result)
    out = pl.pallas_call(
        unpack_kernel,
        grid=(tiles,),
        in_specs=[pl.BlockSpec((400, LANES), lambda i: (i, 0))],
        out_specs=pl.BlockSpec((400, LANES), lambda i: (0, i)),
        out_shape=jax.ShapeDtypeStruct((400, tiles * LANES), f32),
        scratch_shapes=[pltpu.VMEM((LANES, LANES), f32)],
        compiler_params=PARAMS,
        name="unpack",
    )(returned)
    return out.reshape(green_blocks.shape)


def solution(mesh):
    in_specs = (
        P(None, "energy", "momentum", None, None),
        P(None, None, ("energy", "momentum")),
        P(),
        P(),
        P(),
        P(),
    )
    out_specs = P(None, "energy", "momentum", None, None)
    return jax.shard_map(
        on_device, mesh=mesh, in_specs=in_specs, out_specs=out_specs, check_vma=False
    )
```

```python
import jax
import jax.numpy as jnp
import numpy as np
from jax import lax
from jax.experimental import pallas as pl
from jax.experimental.pallas import tpu as pltpu
from jax.sharding import PartitionSpec as P

ORB = 10
PAIRS = ORB * ORB
DEPTH = 112
LANES = 128
ATOMS_HERE = 8
ROWS = 25
POINTS = 128
MODES = 3
AXES = ("energy", "momentum")
HIGHEST = lax.Precision.HIGHEST
constrain = pltpu.with_memory_space_constraint
PARAMS = pltpu.CompilerParams(vmem_limit_bytes=32 * 1024 * 1024)


def split(value):
    high = value.astype(jnp.bfloat16)
    low = (value - high.astype(jnp.float32)).astype(jnp.bfloat16)
    return high, low


def dot(left, right):
    return lax.dot(left, right, preferred_element_type=jnp.float32)


def turn(value, lanes):
    return pltpu.roll(value, lanes % LANES, 1) if lanes % LANES else value


def pack_kernel(green_ref, out_ref, held_ref, rest_ref, sems):
    rest_copy = pltpu.make_async_copy(
        green_ref.at[pl.ds(384, 16), :], held_ref.at[pl.ds(384, 16), :], sems.at[2]
    )
    rest_copy.start()
    copies = []
    for half in range(2):
        place = (pl.ds(0, 384), pl.ds(512 * half, 512))
        copies.append(
            pltpu.make_async_copy(green_ref.at[place], held_ref.at[place], sems.at[half])
        )
        copies[half].start()
    rest_copy.wait()
    rest_ref[...] = jnp.concatenate(
        [held_ref[384:400, LANES * g : LANES * (g + 1)] for g in range(8)], axis=0
    ).T
    lane = lax.broadcasted_iota(jnp.int32, (16, LANES), 1)
    pieces = [rest_ref[pl.ds(atom, 16, stride=8), :] for atom in range(8)]
    for group in range(8):
        joined = None
        for atom in range(8):
            piece = turn(pieces[atom], 16 * (atom - group))
            joined = piece if joined is None else jnp.where(lane < 16 * atom, joined, piece)
        out_ref[pl.ds(400 * group + 24, 16, stride=ROWS), :] = joined
    for group in range(8):
        if group % 4 == 0:
            copies[group // 4].wait()
        for tile in range(3):
            turned = held_ref[
                LANES * tile : LANES * (tile + 1), LANES * group : LANES * (group + 1)
            ].T
            for owner in range(16):
                row = 400 * group + ROWS * owner + 8 * tile
                out_ref[row : row + 8, :] = turned[8 * owner : 8 * owner + 8, :]


def unpack_kernel(in_ref, out_ref, held_ref, rest_ref, sems):
    lane = lax.broadcasted_iota(jnp.int32, (16, LANES), 1)
    pieces = [in_ref[pl.ds(400 * group + 24, 16, stride=ROWS), :] for group in range(8)]
    for atom in range(8):
        joined = None
        for group in range(8):
            piece = turn(pieces[group], 16 * (group - atom))
            joined = piece if joined is None else jnp.where(lane < 16 * group, joined, piece)
        rest_ref[pl.ds(atom, 16, stride=8), :] = joined
    turned = rest_ref[...].T
    for group in range(8):
        held_ref[384:400, LANES * group : LANES * (group + 1)] = turned[
            16 * group : 16 * group + 16, :
        ]
    copies = [
        pltpu.make_async_copy(
            held_ref.at[pl.ds(384, 16), :], out_ref.at[pl.ds(384, 16), :], sems.at[8]
        )
    ]
    copies[0].start()
    for group in range(8):
        for tile in range(3):
            rows = [400 * group + ROWS * owner + 8 * tile for owner in range(16)]
            held_ref[
                LANES * tile : LANES * (tile + 1), LANES * group : LANES * (group + 1)
            ] = jnp.concatenate([in_ref[row : row + 8, :] for row in rows], axis=0).T
        place = (pl.ds(0, 384), pl.ds(LANES * group, LANES))
        copies.append(
            pltpu.make_async_copy(held_ref.at[place], out_ref.at[place], sems.at[group])
        )
        copies[-1].start()
    for copy in copies:
        copy.wait()


def prepare_kernel(
    occ_ref, shift_ref, couple_ref, mix_ref, cols_ref, rows_ref, out_ref, high_ref, low_ref
):
    spread = lax.dot(
        couple_ref[...], cols_ref[...], precision=HIGHEST, preferred_element_type=jnp.float32
    )
    for index in range(ATOMS_HERE * MODES):
        part = spread[16 * index : 16 * index + 16, :]
        first = lax.dot(
            rows_ref[:LANES, :], part[:, :LANES], precision=HIGHEST,
            preferred_element_type=jnp.float32,
        )
        second = lax.dot(
            rows_ref[LANES:, :], part[:, LANES:], precision=HIGHEST,
            preferred_element_type=jnp.float32,
        )
        high, low = split(first * second)
        out_ref[index, :, :LANES] = high[:DEPTH]
        out_ref[index, :, LANES:] = low[:DEPTH]
    row = lax.broadcasted_iota(jnp.int32, (POINTS, POINTS), 0) >> 3
    col = lax.broadcasted_iota(jnp.int32, (POINTS, POINTS), 1) >> 3
    for mode in range(MODES):
        step = shift_ref[mode]
        above = col == row + step
        below = col == row - step
        mixing = mix_ref[mode]
        for kind in range(2):
            upper = occ_ref[mode] + (1.0 - kind)
            lower = occ_ref[mode] + float(kind)
            moved = jnp.where(above, upper, 0.0) + jnp.where(below, lower, 0.0)
            high, low = split(moved * mixing)
            high_ref[kind, POINTS * mode : POINTS * (mode + 1), :] = high
            low_ref[kind, POINTS * mode : POINTS * (mode + 1), :] = low


def compute_kernel(x_ref, weight_ref, high_ref, low_ref, out_ref):
    lane = lax.broadcasted_iota(jnp.int32, (POINTS, LANES), 1)
    rest = x_ref[pl.ds(24, POINTS, stride=ROWS), :]
    rest_out = jnp.zeros((POINTS, LANES), jnp.float32)
    blank = jnp.zeros((LANES - DEPTH, 2 * LANES), jnp.bfloat16)
    for atom in range(ATOMS_HERE):
        tiles = [x_ref[pl.ds(8 * t + atom, POINTS, stride=ROWS), :] for t in range(3)]
        tiles.append(turn(rest, -16 * atom))
        blocks = [tiles[0]]
        for b in range(1, 4):
            joined = jnp.where(lane < PAIRS - 28 * b, tiles[b], tiles[b - 1])
            blocks.append(turn(joined, 28 * b))
        rows = []
        for kind in range(2):
            x_high, x_low = split(jnp.concatenate(blocks[2 * kind : 2 * kind + 2], axis=1))
            table = high_ref[kind]
            moved = dot(
                jnp.concatenate([table, table], axis=1), jnp.concatenate([x_high, x_low], axis=0)
            ) + dot(low_ref[kind], x_high)
            y_high, y_low = split(moved)
            for part in range(2):
                lanes = slice(LANES * part, LANES * (part + 1))
                pieces = []
                for mode in range(MODES):
                    points = slice(POINTS * mode, POINTS * (mode + 1))
                    pieces += [y_high[points, lanes], y_low[points, lanes]]
                rows.append(jnp.concatenate(pieces, axis=1))
        weights = []
        for mode in range(MODES):
            both = jnp.concatenate([weight_ref[MODES * atom + mode], blank], axis=0)
            weights += [both, jnp.concatenate([both[:, :LANES], jnp.zeros_like(both[:, LANES:])], axis=1)]
        result = dot(jnp.concatenate(rows, axis=0), jnp.concatenate(weights, axis=0))
        result = result[:, :LANES] + result[:, LANES:]
        turned = [turn(result[POINTS * b : POINTS * (b + 1)], -28 * b) for b in range(4)]
        for t in range(3):
            out_ref[pl.ds(8 * t + atom, POINTS, stride=ROWS), :] = jnp.where(
                lane < PAIRS - 28 * t, turned[t], turned[t + 1]
            )
        tail = jnp.where(lane < 16, turned[3], 0.0)
        rest_out = rest_out + turn(tail, 16 * atom)
    out_ref[pl.ds(24, POINTS, stride=ROWS), :] = rest_out


def constants():
    pair = np.arange(LANES)
    valid = pair < PAIRS
    cols = np.zeros((LANES, 2 * LANES), np.float32)
    rows = np.zeros((2 * LANES, 16), np.float32)
    for k in range(ORB):
        cols[k, :LANES] = valid & (pair // ORB == k)
        cols[k, LANES:] = valid & (pair % ORB == k)
        rows[:LANES, k] = valid & (pair // ORB == k)
        rows[LANES:, k] = valid & (pair % ORB == k)
    return jnp.asarray(cols), jnp.asarray(rows)


def exchange(message):
    moved = lax.all_to_all(
        message.reshape(POINTS, ROWS, 1, LANES), AXES, split_axis=0, concat_axis=0, tiled=True
    )
    return moved.reshape(POINTS * ROWS, LANES)


def mixing(branch_weight, pair_branch):
    onehot = (
        pair_branch[:, :, None] == jnp.arange(branch_weight.shape[0], dtype=jnp.int32)
    ).astype(jnp.float32)
    return jnp.einsum("kjq,qm->mkj", onehot, branch_weight, precision=HIGHEST)


def on_device(green_blocks, couple_matrix, occupation, energy_shift, branch_weight, pair_branch):
    f32, bf16 = jnp.float32, jnp.bfloat16
    smem = pl.BlockSpec(memory_space=pltpu.SMEM)
    vmem = pl.BlockSpec(memory_space=pltpu.VMEM)
    hbm = pl.BlockSpec(memory_space=pltpu.HBM)
    tiles = green_blocks.shape[4] // LANES
    message = pl.pallas_call(
        pack_kernel,
        in_specs=[hbm],
        out_specs=vmem,
        out_shape=pltpu.VMEM((POINTS * ROWS, LANES), f32),
        scratch_shapes=[
            pltpu.VMEM((400, tiles * LANES), f32),
            pltpu.VMEM((LANES, LANES), f32),
            pltpu.SemaphoreType.DMA((3,)),
        ],
        compiler_params=PARAMS,
        name="pack",
    )(constrain(green_blocks.reshape(400, tiles * LANES), pltpu.HBM))
    received = exchange(message)

    table = jnp.tile(mixing(branch_weight, pair_branch) / pair_branch.shape[0], (1, 16, 16))
    turned = couple_matrix.reshape(MODES, ORB, ORB, ATOMS_HERE).transpose(3, 0, 2, 1)
    turned = jnp.pad(turned, ((0, 0), (0, 0), (0, 6), (0, LANES - ORB))).reshape(-1, LANES)
    cols, rows = constants()
    weight, high, low = pl.pallas_call(
        prepare_kernel,
        in_specs=[smem, smem, vmem, vmem, vmem, vmem],
        out_specs=[vmem, vmem, vmem],
        out_shape=[
            pltpu.VMEM((ATOMS_HERE * MODES, DEPTH, 2 * LANES), bf16),
            pltpu.VMEM((2, MODES * POINTS, POINTS), bf16),
            pltpu.VMEM((2, MODES * POINTS, POINTS), bf16),
        ],
        compiler_params=PARAMS,
        cost_estimate=pl.CostEstimate(flops=10**9, bytes_accessed=4 * 10**6, transcendentals=0),
        name="prepare",
    )(occupation, energy_shift, turned, table, cols, rows)

    result = pl.pallas_call(
        compute_kernel,
        in_specs=[vmem] * 4,
        out_specs=vmem,
        out_shape=pltpu.VMEM((POINTS * ROWS, LANES), f32),
        compiler_params=PARAMS,
        name="compute",
    )(*(constrain(value, pltpu.VMEM) for value in (received, weight, high, low)))
    returned = exchange(result)
    out = pl.pallas_call(
        unpack_kernel,
        in_specs=[vmem],
        out_specs=hbm,
        out_shape=pltpu.HBM((400, tiles * LANES), f32),
        scratch_shapes=[
            pltpu.VMEM((400, tiles * LANES), f32),
            pltpu.VMEM((LANES, LANES), f32),
            pltpu.SemaphoreType.DMA((9,)),
        ],
        compiler_params=PARAMS,
        name="unpack",
    )(constrain(returned, pltpu.VMEM))
    return out.reshape(green_blocks.shape)


def solution(mesh):
    in_specs = (
        P(None, "energy", "momentum", None, None),
        P(None, None, ("energy", "momentum")),
        P(),
        P(),
        P(),
        P(),
    )
    out_specs = P(None, "energy", "momentum", None, None)
    return jax.shard_map(
        on_device, mesh=mesh, in_specs=in_specs, out_specs=out_specs, check_vma=False
    )
```

```python
import jax
import jax.numpy as jnp
import numpy as np
from jax import lax
from jax.experimental import pallas as pl
from jax.experimental.pallas import tpu as pltpu
from jax.sharding import PartitionSpec as P

ORB = 10
PAIRS = ORB * ORB
DEPTH = 112
LANES = 128
ATOMS_HERE = 8
ROWS = 25
POINTS = 128
MODES = 3
AXES = ("energy", "momentum")
HIGHEST = lax.Precision.HIGHEST
constrain = pltpu.with_memory_space_constraint
PARAMS = pltpu.CompilerParams(vmem_limit_bytes=32 * 1024 * 1024)


def split(value):
    high = value.astype(jnp.bfloat16)
    low = (value - high.astype(jnp.float32)).astype(jnp.bfloat16)
    return high, low


def dot(left, right):
    return lax.dot(left, right, preferred_element_type=jnp.float32)


def turn(value, lanes):
    return pltpu.roll(value, lanes % LANES, 1) if lanes % LANES else value


def pack_kernel(green_ref, out_ref, held_ref, message_ref, rest_ref, sems, out_sems):
    rest_copy = pltpu.make_async_copy(
        green_ref.at[pl.ds(384, 16), :], held_ref.at[pl.ds(384, 16), :], sems.at[2]
    )
    rest_copy.start()
    copies = []
    for half in range(2):
        place = (pl.ds(0, 384), pl.ds(512 * half, 512))
        copies.append(
            pltpu.make_async_copy(green_ref.at[place], held_ref.at[place], sems.at[half])
        )
        copies[half].start()
    rest_copy.wait()
    rest_ref[...] = jnp.concatenate(
        [held_ref[384:400, LANES * g : LANES * (g + 1)] for g in range(8)], axis=0
    ).T
    lane = lax.broadcasted_iota(jnp.int32, (16, LANES), 1)
    pieces = [rest_ref[pl.ds(atom, 16, stride=8), :] for atom in range(8)]
    for group in range(8):
        joined = None
        for atom in range(8):
            piece = turn(pieces[atom], 16 * (atom - group))
            joined = piece if joined is None else jnp.where(lane < 16 * atom, joined, piece)
        message_ref[pl.ds(400 * group + 24, 16, stride=ROWS), :] = joined
    for group in range(8):
        if group % 4 == 0:
            copies[group // 4].wait()
        for tile in range(3):
            turned = held_ref[
                LANES * tile : LANES * (tile + 1), LANES * group : LANES * (group + 1)
            ].T
            for owner in range(16):
                row = 400 * group + ROWS * owner + 8 * tile
                message_ref[row : row + 8, :] = turned[8 * owner : 8 * owner + 8, :]
        place = pl.ds(400 * group, 400)
        copies.append(
            pltpu.make_async_copy(message_ref.at[place], out_ref.at[place], out_sems.at[group])
        )
        copies[-1].start()
    for copy in copies[2:]:
        copy.wait()


def unpack_kernel(in_ref, out_ref, held_ref, rest_ref, sems):
    lane = lax.broadcasted_iota(jnp.int32, (16, LANES), 1)
    pieces = [in_ref[pl.ds(400 * group + 24, 16, stride=ROWS), :] for group in range(8)]
    for atom in range(8):
        joined = None
        for group in range(8):
            piece = turn(pieces[group], 16 * (group - atom))
            joined = piece if joined is None else jnp.where(lane < 16 * group, joined, piece)
        rest_ref[pl.ds(atom, 16, stride=8), :] = joined
    turned = rest_ref[...].T
    for group in range(8):
        held_ref[384:400, LANES * group : LANES * (group + 1)] = turned[
            16 * group : 16 * group + 16, :
        ]
    copies = [
        pltpu.make_async_copy(
            held_ref.at[pl.ds(384, 16), :], out_ref.at[pl.ds(384, 16), :], sems.at[8]
        )
    ]
    copies[0].start()
    for group in range(8):
        for tile in range(3):
            rows = [400 * group + ROWS * owner + 8 * tile for owner in range(16)]
            held_ref[
                LANES * tile : LANES * (tile + 1), LANES * group : LANES * (group + 1)
            ] = jnp.concatenate([in_ref[row : row + 8, :] for row in rows], axis=0).T
        place = (pl.ds(0, 384), pl.ds(LANES * group, LANES))
        copies.append(
            pltpu.make_async_copy(held_ref.at[place], out_ref.at[place], sems.at[group])
        )
        copies[-1].start()
    for copy in copies:
        copy.wait()


def prepare_kernel(
    occ_ref, shift_ref, couple_ref, mix_ref, cols_ref, rows_ref, out_ref, high_ref, low_ref
):
    spread = lax.dot(
        couple_ref[...], cols_ref[...], precision=HIGHEST, preferred_element_type=jnp.float32
    )
    for index in range(ATOMS_HERE * MODES):
        part = spread[16 * index : 16 * index + 16, :]
        first = lax.dot(
            rows_ref[:LANES, :], part[:, :LANES], precision=HIGHEST,
            preferred_element_type=jnp.float32,
        )
        second = lax.dot(
            rows_ref[LANES:, :], part[:, LANES:], precision=HIGHEST,
            preferred_element_type=jnp.float32,
        )
        high, low = split(first * second)
        out_ref[index, :, :LANES] = high[:DEPTH]
        out_ref[index, :, LANES:] = low[:DEPTH]
    row = lax.broadcasted_iota(jnp.int32, (POINTS, POINTS), 0) >> 3
    col = lax.broadcasted_iota(jnp.int32, (POINTS, POINTS), 1) >> 3
    for mode in range(MODES):
        step = shift_ref[mode]
        above = col == row + step
        below = col == row - step
        mixing = mix_ref[mode]
        for kind in range(2):
            upper = occ_ref[mode] + (1.0 - kind)
            lower = occ_ref[mode] + float(kind)
            moved = jnp.where(above, upper, 0.0) + jnp.where(below, lower, 0.0)
            high, low = split(moved * mixing)
            high_ref[kind, POINTS * mode : POINTS * (mode + 1), :] = high
            low_ref[kind, POINTS * mode : POINTS * (mode + 1), :] = low


def compute_kernel(x_ref, weight_ref, high_ref, low_ref, out_ref):
    lane = lax.broadcasted_iota(jnp.int32, (POINTS, LANES), 1)
    rest = x_ref[pl.ds(24, POINTS, stride=ROWS), :]
    blank = jnp.zeros((LANES - DEPTH, 2 * LANES), jnp.bfloat16)

    def shifted(atom):
        tiles = [x_ref[pl.ds(8 * t + atom, POINTS, stride=ROWS), :] for t in range(3)]
        tiles.append(turn(rest, -16 * atom))
        blocks = [tiles[0]]
        for b in range(1, 4):
            joined = jnp.where(lane < PAIRS - 28 * b, tiles[b], tiles[b - 1])
            blocks.append(turn(joined, 28 * b))
        parts = []
        for kind in range(2):
            x_high, x_low = split(jnp.concatenate(blocks[2 * kind : 2 * kind + 2], axis=1))
            table = high_ref[kind]
            moved = dot(
                jnp.concatenate([table, table], axis=1), jnp.concatenate([x_high, x_low], axis=0)
            ) + dot(low_ref[kind], x_high)
            parts.append(split(moved))
        return parts

    def sandwiched(atom, parts):
        rows = []
        for high, low in parts:
            for part in range(2):
                lanes = slice(LANES * part, LANES * (part + 1))
                pieces = []
                for mode in range(MODES):
                    points = slice(POINTS * mode, POINTS * (mode + 1))
                    pieces += [high[points, lanes], low[points, lanes]]
                rows.append(jnp.concatenate(pieces, axis=1))
        weights = []
        for mode in range(MODES):
            both = jnp.concatenate([weight_ref[MODES * atom + mode], blank], axis=0)
            weights += [
                both,
                jnp.concatenate([both[:, :LANES], jnp.zeros_like(both[:, LANES:])], axis=1),
            ]
        result = dot(jnp.concatenate(rows, axis=0), jnp.concatenate(weights, axis=0))
        return result[:, :LANES] + result[:, LANES:]

    rest_out = jnp.zeros((POINTS, LANES), jnp.float32)
    parts = shifted(0)
    for atom in range(ATOMS_HERE):
        following = shifted(atom + 1) if atom + 1 < ATOMS_HERE else None
        result = sandwiched(atom, parts)
        turned = [turn(result[POINTS * b : POINTS * (b + 1)], -28 * b) for b in range(4)]
        for t in range(3):
            out_ref[pl.ds(8 * t + atom, POINTS, stride=ROWS), :] = jnp.where(
                lane < PAIRS - 28 * t, turned[t], turned[t + 1]
            )
        rest_out = rest_out + turn(jnp.where(lane < 16, turned[3], 0.0), 16 * atom)
        parts = following
    out_ref[pl.ds(24, POINTS, stride=ROWS), :] = rest_out


def constants():
    pair = np.arange(LANES)
    valid = pair < PAIRS
    cols = np.zeros((LANES, 2 * LANES), np.float32)
    rows = np.zeros((2 * LANES, 16), np.float32)
    for k in range(ORB):
        cols[k, :LANES] = valid & (pair // ORB == k)
        cols[k, LANES:] = valid & (pair % ORB == k)
        rows[:LANES, k] = valid & (pair // ORB == k)
        rows[LANES:, k] = valid & (pair % ORB == k)
    return jnp.asarray(cols), jnp.asarray(rows)


def exchange(message):
    moved = lax.all_to_all(
        message.reshape(POINTS, ROWS, 1, LANES), AXES, split_axis=0, concat_axis=0, tiled=True
    )
    return moved.reshape(POINTS * ROWS, LANES)


def mixing(branch_weight, pair_branch):
    onehot = (
        pair_branch[:, :, None] == jnp.arange(branch_weight.shape[0], dtype=jnp.int32)
    ).astype(jnp.float32)
    return jnp.einsum("kjq,qm->mkj", onehot, branch_weight, precision=HIGHEST)


def on_device(green_blocks, couple_matrix, occupation, energy_shift, branch_weight, pair_branch):
    f32, bf16 = jnp.float32, jnp.bfloat16
    smem = pl.BlockSpec(memory_space=pltpu.SMEM)
    vmem = pl.BlockSpec(memory_space=pltpu.VMEM)
    hbm = pl.BlockSpec(memory_space=pltpu.HBM)
    tiles = green_blocks.shape[4] // LANES
    message = pl.pallas_call(
        pack_kernel,
        in_specs=[hbm],
        out_specs=hbm,
        out_shape=pltpu.HBM((POINTS * ROWS, LANES), f32),
        scratch_shapes=[
            pltpu.VMEM((400, tiles * LANES), f32),
            pltpu.VMEM((POINTS * ROWS, LANES), f32),
            pltpu.VMEM((LANES, LANES), f32),
            pltpu.SemaphoreType.DMA((3,)),
            pltpu.SemaphoreType.DMA((8,)),
        ],
        compiler_params=PARAMS,
        name="pack",
    )(constrain(green_blocks.reshape(400, tiles * LANES), pltpu.HBM))
    received = exchange(message)

    table = jnp.tile(mixing(branch_weight, pair_branch) / pair_branch.shape[0], (1, 16, 16))
    turned = couple_matrix.reshape(MODES, ORB, ORB, ATOMS_HERE).transpose(3, 0, 2, 1)
    turned = jnp.pad(turned, ((0, 0), (0, 0), (0, 6), (0, LANES - ORB))).reshape(-1, LANES)
    cols, rows = constants()
    weight, high, low = pl.pallas_call(
        prepare_kernel,
        in_specs=[smem, smem, vmem, vmem, vmem, vmem],
        out_specs=[vmem, vmem, vmem],
        out_shape=[
            pltpu.VMEM((ATOMS_HERE * MODES, DEPTH, 2 * LANES), bf16),
            pltpu.VMEM((2, MODES * POINTS, POINTS), bf16),
            pltpu.VMEM((2, MODES * POINTS, POINTS), bf16),
        ],
        compiler_params=PARAMS,
        cost_estimate=pl.CostEstimate(flops=10**9, bytes_accessed=4 * 10**6, transcendentals=0),
        name="prepare",
    )(occupation, energy_shift, turned, table, cols, rows)

    result = pl.pallas_call(
        compute_kernel,
        in_specs=[vmem] * 4,
        out_specs=vmem,
        out_shape=pltpu.VMEM((POINTS * ROWS, LANES), f32),
        compiler_params=PARAMS,
        name="compute",
    )(*(constrain(value, pltpu.VMEM) for value in (received, weight, high, low)))
    returned = exchange(result)
    out = pl.pallas_call(
        unpack_kernel,
        in_specs=[vmem],
        out_specs=hbm,
        out_shape=pltpu.HBM((400, tiles * LANES), f32),
        scratch_shapes=[
            pltpu.VMEM((400, tiles * LANES), f32),
            pltpu.VMEM((LANES, LANES), f32),
            pltpu.SemaphoreType.DMA((9,)),
        ],
        compiler_params=PARAMS,
        name="unpack",
    )(constrain(returned, pltpu.VMEM))
    return out.reshape(green_blocks.shape)


def solution(mesh):
    in_specs = (
        P(None, "energy", "momentum", None, None),
        P(None, None, ("energy", "momentum")),
        P(),
        P(),
        P(),
        P(),
    )
    out_specs = P(None, "energy", "momentum", None, None)
    return jax.shard_map(
        on_device, mesh=mesh, in_specs=in_specs, out_specs=out_specs, check_vma=False
    )
```

```python
import functools

import jax
import jax.numpy as jnp
import numpy as np
from jax import lax
from jax.experimental import pallas as pl
from jax.experimental.pallas import tpu as pltpu
from jax.sharding import PartitionSpec as P

ORB = 10
PAIRS = ORB * ORB
DEPTH = 112
LANES = 128
ATOMS_HERE = 8
ROWS = 25
POINTS = 128
MODES = 3
AXES = ("energy", "momentum")
HIGHEST = lax.Precision.HIGHEST
constrain = pltpu.with_memory_space_constraint
PARAMS = pltpu.CompilerParams(vmem_limit_bytes=32 * 1024 * 1024)


def split(value):
    high = value.astype(jnp.bfloat16)
    low = (value - high.astype(jnp.float32)).astype(jnp.bfloat16)
    return high, low


def dot(left, right):
    return lax.dot(left, right, preferred_element_type=jnp.float32)


def turn(value, lanes):
    return pltpu.roll(value, lanes % LANES, 1) if lanes % LANES else value


def pack_kernel(spots, green_ref, out_ref, held_ref, message_ref, rest_ref, sems, out_sems):
    rest_copy = pltpu.make_async_copy(
        green_ref.at[pl.ds(384, 16), :], held_ref.at[pl.ds(384, 16), :], sems.at[2]
    )
    rest_copy.start()
    copies = []
    for part in range(2):
        place = (pl.ds(0, 384), pl.ds(512 * part, 512))
        copies.append(
            pltpu.make_async_copy(green_ref.at[place], held_ref.at[place], sems.at[part])
        )
        copies[part].start()
    rest_copy.wait()
    rest_ref[...] = jnp.concatenate(
        [held_ref[384:400, LANES * g : LANES * (g + 1)] for g in range(8)], axis=0
    ).T
    lane = lax.broadcasted_iota(jnp.int32, (16, LANES), 1)
    pieces = [rest_ref[pl.ds(atom, 16, stride=8), :] for atom in range(8)]
    for group in range(8):
        joined = None
        for atom in range(8):
            piece = turn(pieces[atom], 16 * (atom - group))
            joined = piece if joined is None else jnp.where(lane < 16 * atom, joined, piece)
        for first in range(0, 16, 4):
            row = ROWS * spots[16 * group + first] + 24
            message_ref[pl.ds(row, 4, stride=ROWS), :] = joined[first : first + 4, :]
    waited, filled, sent = set(), [0] * 8, []
    for group in (0, 2, 4, 6, 1, 3, 5, 7):
        if group // 4 not in waited:
            copies[group // 4].wait()
            waited.add(group // 4)
        for tile in range(3):
            turned = held_ref[
                LANES * tile : LANES * (tile + 1), LANES * group : LANES * (group + 1)
            ].T
            for owner in range(16):
                row = ROWS * spots[16 * group + owner] + 8 * tile
                message_ref[row : row + 8, :] = turned[8 * owner : 8 * owner + 8, :]
        for owner in range(16):
            block = spots[16 * group + owner] // 16
            filled[block] += 1
            if filled[block] == 16:
                place = pl.ds(400 * block, 400)
                sent.append(
                    pltpu.make_async_copy(
                        message_ref.at[place], out_ref.at[place], out_sems.at[block]
                    )
                )
                sent[-1].start()
    for copy in sent:
        copy.wait()


def unpack_kernel(spots, in_ref, out_ref, held_ref, rest_ref, sems):
    lane = lax.broadcasted_iota(jnp.int32, (16, LANES), 1)
    pieces = []
    for group in range(8):
        rows = [ROWS * spots[16 * group + first] + 24 for first in range(0, 16, 4)]
        pieces.append(
            jnp.concatenate([in_ref[pl.ds(row, 4, stride=ROWS), :] for row in rows], axis=0)
        )
    for atom in range(8):
        joined = None
        for group in range(8):
            piece = turn(pieces[group], 16 * (group - atom))
            joined = piece if joined is None else jnp.where(lane < 16 * group, joined, piece)
        rest_ref[pl.ds(atom, 16, stride=8), :] = joined
    turned = rest_ref[...].T
    for group in range(8):
        held_ref[384:400, LANES * group : LANES * (group + 1)] = turned[
            16 * group : 16 * group + 16, :
        ]
    copies = [
        pltpu.make_async_copy(
            held_ref.at[pl.ds(384, 16), :], out_ref.at[pl.ds(384, 16), :], sems.at[8]
        )
    ]
    copies[0].start()
    for group in range(8):
        for tile in range(3):
            rows = [ROWS * spots[16 * group + owner] + 8 * tile for owner in range(16)]
            held_ref[
                LANES * tile : LANES * (tile + 1), LANES * group : LANES * (group + 1)
            ] = jnp.concatenate([in_ref[row : row + 8, :] for row in rows], axis=0).T
        place = (pl.ds(0, 384), pl.ds(LANES * group, LANES))
        copies.append(
            pltpu.make_async_copy(held_ref.at[place], out_ref.at[place], sems.at[group])
        )
        copies[-1].start()
    for copy in copies:
        copy.wait()


def prepare_kernel(
    occ_ref,
    shift_ref,
    couple_ref,
    mix_ref,
    cols_ref,
    rows_ref,
    pick_ref,
    picked_ref,
    row_ref,
    col_ref,
    out_ref,
    high_ref,
    low_ref,
):
    spread = lax.dot(
        couple_ref[...], cols_ref[...], precision=HIGHEST, preferred_element_type=jnp.float32
    )
    for index in range(ATOMS_HERE * MODES):
        part = spread[16 * index : 16 * index + 16, :]
        first = lax.dot(
            rows_ref[:LANES, :], part[:, :LANES], precision=HIGHEST,
            preferred_element_type=jnp.float32,
        )
        second = lax.dot(
            rows_ref[LANES:, :], part[:, LANES:], precision=HIGHEST,
            preferred_element_type=jnp.float32,
        )
        high, low = split(first * second)
        out_ref[index, :, :LANES] = high[:DEPTH]
        out_ref[index, :, LANES:] = low[:DEPTH]
    row = jnp.broadcast_to(row_ref[...], (POINTS, POINTS))
    col = jnp.broadcast_to(col_ref[...], (POINTS, POINTS))
    for mode in range(MODES):
        step = shift_ref[mode]
        above = col == row + step
        below = col == row - step
        mixing = lax.dot(
            lax.dot(
                pick_ref[:, :8], mix_ref[mode], precision=HIGHEST,
                preferred_element_type=jnp.float32,
            ),
            picked_ref[...], precision=HIGHEST, preferred_element_type=jnp.float32,
        )
        for kind in range(2):
            upper = occ_ref[mode] + (1.0 - kind)
            lower = occ_ref[mode] + float(kind)
            moved = jnp.where(above, upper, 0.0) + jnp.where(below, lower, 0.0)
            high, low = split(moved * mixing)
            high_ref[kind, POINTS * mode : POINTS * (mode + 1), :] = high
            low_ref[kind, POINTS * mode : POINTS * (mode + 1), :] = low


def compute_kernel(x_ref, weight_ref, high_ref, low_ref, out_ref):
    lane = lax.broadcasted_iota(jnp.int32, (POINTS, LANES), 1)
    rest = x_ref[pl.ds(24, POINTS, stride=ROWS), :]
    blank = jnp.zeros((LANES - DEPTH, 2 * LANES), jnp.bfloat16)

    def shifted(atom):
        tiles = [x_ref[pl.ds(8 * t + atom, POINTS, stride=ROWS), :] for t in range(3)]
        tiles.append(turn(rest, -16 * atom))
        blocks = [tiles[0]]
        for b in range(1, 4):
            joined = jnp.where(lane < PAIRS - 28 * b, tiles[b], tiles[b - 1])
            blocks.append(turn(joined, 28 * b))
        parts = []
        for kind in range(2):
            x_high, x_low = split(jnp.concatenate(blocks[2 * kind : 2 * kind + 2], axis=1))
            table = high_ref[kind]
            moved = dot(
                jnp.concatenate([table, table], axis=1), jnp.concatenate([x_high, x_low], axis=0)
            ) + dot(low_ref[kind], x_high)
            parts.append(split(moved))
        return parts

    def sandwiched(atom, parts):
        rows = []
        for high, low in parts:
            for part in range(2):
                lanes = slice(LANES * part, LANES * (part + 1))
                pieces = []
                for mode in range(MODES):
                    points = slice(POINTS * mode, POINTS * (mode + 1))
                    pieces += [high[points, lanes], low[points, lanes]]
                rows.append(jnp.concatenate(pieces, axis=1))
        weights = []
        for mode in range(MODES):
            both = jnp.concatenate([weight_ref[MODES * atom + mode], blank], axis=0)
            weights += [
                both,
                jnp.concatenate([both[:, :LANES], jnp.zeros_like(both[:, LANES:])], axis=1),
            ]
        result = dot(jnp.concatenate(rows, axis=0), jnp.concatenate(weights, axis=0))
        return result[:, :LANES] + result[:, LANES:]

    rest_out = jnp.zeros((POINTS, LANES), jnp.float32)
    parts = shifted(0)
    for atom in range(ATOMS_HERE):
        following = shifted(atom + 1) if atom + 1 < ATOMS_HERE else None
        result = sandwiched(atom, parts)
        turned = [turn(result[POINTS * b : POINTS * (b + 1)], -28 * b) for b in range(4)]
        for t in range(3):
            out_ref[pl.ds(8 * t + atom, POINTS, stride=ROWS), :] = jnp.where(
                lane < PAIRS - 28 * t, turned[t], turned[t + 1]
            )
        rest_out = rest_out + turn(jnp.where(lane < 16, turned[3], 0.0), 16 * atom)
        parts = following
    out_ref[pl.ds(24, POINTS, stride=ROWS), :] = rest_out


def constants():
    pair = np.arange(LANES)
    valid = pair < PAIRS
    cols = np.zeros((LANES, 2 * LANES), np.float32)
    rows = np.zeros((2 * LANES, 16), np.float32)
    for k in range(ORB):
        cols[k, :LANES] = valid & (pair // ORB == k)
        cols[k, LANES:] = valid & (pair % ORB == k)
        rows[:LANES, k] = valid & (pair // ORB == k)
        rows[LANES:, k] = valid & (pair % ORB == k)
    return jnp.asarray(cols), jnp.asarray(rows)


def exchange(message, order):
    moved = lax.all_to_all(
        message.reshape(POINTS, ROWS, 1, LANES),
        AXES,
        split_axis=0,
        concat_axis=0,
        tiled=True,
        axis_index_groups=[order],
    )
    return moved.reshape(POINTS * ROWS, LANES)


def mixing(branch_weight, pair_branch):
    onehot = (
        pair_branch[:, :, None] == jnp.arange(branch_weight.shape[0], dtype=jnp.int32)
    ).astype(jnp.float32)
    return jnp.einsum("kjq,qm->mkj", onehot, branch_weight, precision=HIGHEST)


def on_device(
    order, green_blocks, couple_matrix, occupation, energy_shift, branch_weight, pair_branch
):
    f32, bf16 = jnp.float32, jnp.bfloat16
    spots = [order.index(device) for device in range(POINTS)]
    smem = pl.BlockSpec(memory_space=pltpu.SMEM)
    vmem = pl.BlockSpec(memory_space=pltpu.VMEM)
    hbm = pl.BlockSpec(memory_space=pltpu.HBM)
    tiles = green_blocks.shape[4] // LANES
    message = pl.pallas_call(
        functools.partial(pack_kernel, spots),
        in_specs=[hbm],
        out_specs=hbm,
        out_shape=pltpu.HBM((POINTS * ROWS, LANES), f32),
        scratch_shapes=[
            pltpu.VMEM((400, tiles * LANES), f32),
            pltpu.VMEM((POINTS * ROWS, LANES), f32),
            pltpu.VMEM((LANES, LANES), f32),
            pltpu.SemaphoreType.DMA((3,)),
            pltpu.SemaphoreType.DMA((8,)),
        ],
        compiler_params=PARAMS,
        name="pack",
    )(constrain(green_blocks.reshape(400, tiles * LANES), pltpu.HBM))
    received = exchange(message, order)

    moments = pair_branch.shape[0]
    energies = jnp.asarray([place // moments for place in order], jnp.int32)
    pick = np.zeros((POINTS, moments), np.float32)
    pick[np.arange(POINTS), [place % moments for place in order]] = 1.0
    table = mixing(branch_weight, pair_branch) / moments
    turned = couple_matrix.reshape(MODES, ORB, ORB, ATOMS_HERE).transpose(3, 0, 2, 1)
    turned = jnp.pad(turned, ((0, 0), (0, 0), (0, 6), (0, LANES - ORB))).reshape(-1, LANES)
    cols, rows = constants()
    weight, high, low = pl.pallas_call(
        prepare_kernel,
        in_specs=[smem, smem] + [vmem] * 8,
        out_specs=[vmem, vmem, vmem],
        out_shape=[
            pltpu.VMEM((ATOMS_HERE * MODES, DEPTH, 2 * LANES), bf16),
            pltpu.VMEM((2, MODES * POINTS, POINTS), bf16),
            pltpu.VMEM((2, MODES * POINTS, POINTS), bf16),
        ],
        compiler_params=PARAMS,
        cost_estimate=pl.CostEstimate(flops=10**9, bytes_accessed=4 * 10**6, transcendentals=0),
        name="prepare",
    )(
        occupation,
        energy_shift,
        turned,
        jnp.pad(table, ((0, 0), (0, 0), (0, LANES - moments))),
        cols,
        rows,
        jnp.asarray(np.pad(pick, ((0, 0), (0, LANES - moments)))),
        jnp.asarray(np.pad(pick.T, ((0, LANES - moments), (0, 0)))),
        energies[:, None],
        energies[None, :],
    )

    result = pl.pallas_call(
        compute_kernel,
        in_specs=[vmem] * 4,
        out_specs=vmem,
        out_shape=pltpu.VMEM((POINTS * ROWS, LANES), f32),
        compiler_params=PARAMS,
        name="compute",
    )(*(constrain(value, pltpu.VMEM) for value in (received, weight, high, low)))
    returned = exchange(result, order)
    out = pl.pallas_call(
        functools.partial(unpack_kernel, spots),
        in_specs=[vmem],
        out_specs=hbm,
        out_shape=pltpu.HBM((400, tiles * LANES), f32),
        scratch_shapes=[
            pltpu.VMEM((400, tiles * LANES), f32),
            pltpu.VMEM((LANES, LANES), f32),
            pltpu.SemaphoreType.DMA((9,)),
        ],
        compiler_params=PARAMS,
        name="unpack",
    )(constrain(returned, pltpu.VMEM))
    return out.reshape(green_blocks.shape)


def places(mesh):
    def key(place):
        energy, momentum = divmod(place, 8)
        z = 2 * (momentum // 4) + (energy // 2) % 2
        return energy % 2, z, energy // 4, momentum % 4

    return sorted(range(mesh.size), key=key)


def solution(mesh):
    in_specs = (
        P(None, "energy", "momentum", None, None),
        P(None, None, ("energy", "momentum")),
        P(),
        P(),
        P(),
        P(),
    )
    out_specs = P(None, "energy", "momentum", None, None)
    order = places(mesh)
    return jax.shard_map(
        functools.partial(on_device, order), mesh=mesh, in_specs=in_specs, out_specs=out_specs, check_vma=False
    )
```

```python
import functools

import jax
import jax.numpy as jnp
import numpy as np
from jax import lax
from jax.experimental import pallas as pl
from jax.experimental.pallas import tpu as pltpu
from jax.sharding import PartitionSpec as P

ORB = 10
PAIRS = ORB * ORB
DEPTH = 112
LANES = 128
ATOMS_HERE = 8
ROWS = 25
POINTS = 128
MODES = 3
AXES = ("energy", "momentum")
HIGHEST = lax.Precision.HIGHEST
constrain = pltpu.with_memory_space_constraint
PARAMS = pltpu.CompilerParams(vmem_limit_bytes=32 * 1024 * 1024)


def split(value):
    high = value.astype(jnp.bfloat16)
    low = (value - high.astype(jnp.float32)).astype(jnp.bfloat16)
    return high, low


def dot(left, right):
    return lax.dot(left, right, preferred_element_type=jnp.float32)


def turn(value, lanes):
    return pltpu.roll(value, lanes % LANES, 1) if lanes % LANES else value


def pack_kernel(spots, green_ref, out_ref, held_ref, message_ref, rest_ref, sems, out_sems):
    rest_copy = pltpu.make_async_copy(
        green_ref.at[pl.ds(384, 16), :], held_ref.at[pl.ds(384, 16), :], sems.at[2]
    )
    rest_copy.start()
    copies = []
    for part in range(2):
        place = (pl.ds(0, 384), pl.ds(512 * part, 512))
        copies.append(
            pltpu.make_async_copy(green_ref.at[place], held_ref.at[place], sems.at[part])
        )
        copies[part].start()
    rest_copy.wait()
    rest_ref[...] = jnp.concatenate(
        [held_ref[384:400, LANES * g : LANES * (g + 1)] for g in range(8)], axis=0
    ).T
    lane = lax.broadcasted_iota(jnp.int32, (16, LANES), 1)
    pieces = [rest_ref[pl.ds(atom, 16, stride=8), :] for atom in range(8)]
    for group in range(8):
        joined = None
        for atom in range(8):
            piece = turn(pieces[atom], 16 * (atom - group))
            joined = piece if joined is None else jnp.where(lane < 16 * atom, joined, piece)
        for first in range(0, 16, 4):
            row = ROWS * spots[16 * group + first] + 24
            message_ref[pl.ds(row, 4, stride=ROWS), :] = joined[first : first + 4, :]
    waited, filled, sent = set(), [0] * 8, []
    for group in (0, 2, 4, 6, 1, 3, 5, 7):
        if group // 4 not in waited:
            copies[group // 4].wait()
            waited.add(group // 4)
        for tile in range(3):
            turned = held_ref[
                LANES * tile : LANES * (tile + 1), LANES * group : LANES * (group + 1)
            ].T
            for owner in range(16):
                row = ROWS * spots[16 * group + owner] + 8 * tile
                message_ref[row : row + 8, :] = turned[8 * owner : 8 * owner + 8, :]
        for owner in range(16):
            block = spots[16 * group + owner] // 16
            filled[block] += 1
            if filled[block] == 16:
                place = pl.ds(400 * block, 400)
                sent.append(
                    pltpu.make_async_copy(
                        message_ref.at[place], out_ref.at[place], out_sems.at[block]
                    )
                )
                sent[-1].start()
    for copy in sent:
        copy.wait()


def unpack_kernel(spots, in_ref, out_ref, held_ref, rest_ref, sems):
    lane = lax.broadcasted_iota(jnp.int32, (16, LANES), 1)
    pieces = []
    for group in range(8):
        rows = [ROWS * spots[16 * group + first] + 24 for first in range(0, 16, 4)]
        step = ROWS * (spots[1] - spots[0])
        pieces.append(
            jnp.concatenate([in_ref[pl.ds(row, 4, stride=step), :] for row in rows], axis=0)
        )
    for atom in range(8):
        joined = None
        for group in range(8):
            piece = turn(pieces[group], 16 * (group - atom))
            joined = piece if joined is None else jnp.where(lane < 16 * group, joined, piece)
        rest_ref[pl.ds(atom, 16, stride=8), :] = joined
    turned = rest_ref[...].T
    for group in range(8):
        held_ref[384:400, LANES * group : LANES * (group + 1)] = turned[
            16 * group : 16 * group + 16, :
        ]
    copies = [
        pltpu.make_async_copy(
            held_ref.at[pl.ds(384, 16), :], out_ref.at[pl.ds(384, 16), :], sems.at[8]
        )
    ]
    copies[0].start()
    for group in range(8):
        for tile in range(3):
            rows = [ROWS * spots[16 * group + owner] + 8 * tile for owner in range(16)]
            held_ref[
                LANES * tile : LANES * (tile + 1), LANES * group : LANES * (group + 1)
            ] = jnp.concatenate([in_ref[row : row + 8, :] for row in rows], axis=0).T
        place = (pl.ds(0, 384), pl.ds(LANES * group, LANES))
        copies.append(
            pltpu.make_async_copy(held_ref.at[place], out_ref.at[place], sems.at[group])
        )
        copies[-1].start()
    for copy in copies:
        copy.wait()


def prepare_kernel(
    occ_ref,
    shift_ref,
    couple_ref,
    mix_ref,
    cols_ref,
    rows_ref,
    pick_ref,
    picked_ref,
    row_ref,
    col_ref,
    out_ref,
    high_ref,
    low_ref,
):
    spread = lax.dot(
        couple_ref[...], cols_ref[...], precision=HIGHEST, preferred_element_type=jnp.float32
    )
    for index in range(ATOMS_HERE * MODES):
        part = spread[16 * index : 16 * index + 16, :]
        first = lax.dot(
            rows_ref[:LANES, :], part[:, :LANES], precision=HIGHEST,
            preferred_element_type=jnp.float32,
        )
        second = lax.dot(
            rows_ref[LANES:, :], part[:, LANES:], precision=HIGHEST,
            preferred_element_type=jnp.float32,
        )
        high, low = split(first * second)
        out_ref[index, :, :LANES] = high[:DEPTH]
        out_ref[index, :, LANES:] = low[:DEPTH]
    row = jnp.broadcast_to(row_ref[...], (POINTS, POINTS))
    col = jnp.broadcast_to(col_ref[...], (POINTS, POINTS))
    for mode in range(MODES):
        step = shift_ref[mode]
        above = col == row + step
        below = col == row - step
        mixing = lax.dot(
            lax.dot(
                pick_ref[:, :8], mix_ref[mode], precision=HIGHEST,
                preferred_element_type=jnp.float32,
            ),
            picked_ref[...], precision=HIGHEST, preferred_element_type=jnp.float32,
        )
        for kind in range(2):
            upper = occ_ref[mode] + (1.0 - kind)
            lower = occ_ref[mode] + float(kind)
            moved = jnp.where(above, upper, 0.0) + jnp.where(below, lower, 0.0)
            high, low = split(moved * mixing)
            high_ref[kind, POINTS * mode : POINTS * (mode + 1), :] = high
            low_ref[kind, POINTS * mode : POINTS * (mode + 1), :] = low


def compute_kernel(x_ref, weight_ref, high_ref, low_ref, out_ref):
    lane = lax.broadcasted_iota(jnp.int32, (POINTS, LANES), 1)
    rest = x_ref[pl.ds(24, POINTS, stride=ROWS), :]
    blank = jnp.zeros((LANES - DEPTH, 2 * LANES), jnp.bfloat16)

    def shifted(atom):
        tiles = [x_ref[pl.ds(8 * t + atom, POINTS, stride=ROWS), :] for t in range(3)]
        tiles.append(turn(rest, -16 * atom))
        blocks = [tiles[0]]
        for b in range(1, 4):
            joined = jnp.where(lane < PAIRS - 28 * b, tiles[b], tiles[b - 1])
            blocks.append(turn(joined, 28 * b))
        parts = []
        for kind in range(2):
            x_high, x_low = split(jnp.concatenate(blocks[2 * kind : 2 * kind + 2], axis=1))
            table = high_ref[kind]
            moved = dot(
                jnp.concatenate([table, table], axis=1), jnp.concatenate([x_high, x_low], axis=0)
            ) + dot(low_ref[kind], x_high)
            parts.append(split(moved))
        return parts

    def sandwiched(atom, parts):
        rows = []
        for high, low in parts:
            for part in range(2):
                lanes = slice(LANES * part, LANES * (part + 1))
                pieces = []
                for mode in range(MODES):
                    points = slice(POINTS * mode, POINTS * (mode + 1))
                    pieces += [high[points, lanes], low[points, lanes]]
                rows.append(jnp.concatenate(pieces, axis=1))
        weights = []
        for mode in range(MODES):
            both = jnp.concatenate([weight_ref[MODES * atom + mode], blank], axis=0)
            weights += [
                both,
                jnp.concatenate([both[:, :LANES], jnp.zeros_like(both[:, LANES:])], axis=1),
            ]
        result = dot(jnp.concatenate(rows, axis=0), jnp.concatenate(weights, axis=0))
        return result[:, :LANES] + result[:, LANES:]

    rest_out = jnp.zeros((POINTS, LANES), jnp.float32)
    parts = shifted(0)
    for atom in range(ATOMS_HERE):
        following = shifted(atom + 1) if atom + 1 < ATOMS_HERE else None
        result = sandwiched(atom, parts)
        turned = [turn(result[POINTS * b : POINTS * (b + 1)], -28 * b) for b in range(4)]
        for t in range(3):
            out_ref[pl.ds(8 * t + atom, POINTS, stride=ROWS), :] = jnp.where(
                lane < PAIRS - 28 * t, turned[t], turned[t + 1]
            )
        rest_out = rest_out + turn(jnp.where(lane < 16, turned[3], 0.0), 16 * atom)
        parts = following
    out_ref[pl.ds(24, POINTS, stride=ROWS), :] = rest_out


def constants():
    pair = np.arange(LANES)
    valid = pair < PAIRS
    cols = np.zeros((LANES, 2 * LANES), np.float32)
    rows = np.zeros((2 * LANES, 16), np.float32)
    for k in range(ORB):
        cols[k, :LANES] = valid & (pair // ORB == k)
        cols[k, LANES:] = valid & (pair % ORB == k)
        rows[:LANES, k] = valid & (pair // ORB == k)
        rows[LANES:, k] = valid & (pair % ORB == k)
    return jnp.asarray(cols), jnp.asarray(rows)


def exchange(message, order):
    moved = lax.all_to_all(
        message.reshape(POINTS, ROWS, 1, LANES),
        AXES,
        split_axis=0,
        concat_axis=0,
        tiled=True,
        axis_index_groups=[order],
    )
    return moved.reshape(POINTS * ROWS, LANES)


def mixing(branch_weight, pair_branch):
    onehot = (
        pair_branch[:, :, None] == jnp.arange(branch_weight.shape[0], dtype=jnp.int32)
    ).astype(jnp.float32)
    return jnp.einsum("kjq,qm->mkj", onehot, branch_weight, precision=HIGHEST)


def on_device(
    out_order, back_order, green_blocks, couple_matrix, occupation, energy_shift, branch_weight, pair_branch
):
    f32, bf16 = jnp.float32, jnp.bfloat16
    out_spots = [out_order.index(device) for device in range(POINTS)]
    back_spots = [back_order.index(device) for device in range(POINTS)]
    smem = pl.BlockSpec(memory_space=pltpu.SMEM)
    vmem = pl.BlockSpec(memory_space=pltpu.VMEM)
    hbm = pl.BlockSpec(memory_space=pltpu.HBM)
    tiles = green_blocks.shape[4] // LANES
    message = pl.pallas_call(
        functools.partial(pack_kernel, out_spots),
        in_specs=[hbm],
        out_specs=hbm,
        out_shape=pltpu.HBM((POINTS * ROWS, LANES), f32),
        scratch_shapes=[
            pltpu.VMEM((400, tiles * LANES), f32),
            pltpu.VMEM((POINTS * ROWS, LANES), f32),
            pltpu.VMEM((LANES, LANES), f32),
            pltpu.SemaphoreType.DMA((3,)),
            pltpu.SemaphoreType.DMA((8,)),
        ],
        compiler_params=PARAMS,
        name="pack",
    )(constrain(green_blocks.reshape(400, tiles * LANES), pltpu.HBM))
    received = exchange(message, out_order)

    moments = pair_branch.shape[0]
    picks, energies = [], []
    for order in (back_order, out_order):
        pick = np.zeros((POINTS, moments), np.float32)
        pick[np.arange(POINTS), [place % moments for place in order]] = 1.0
        picks.append(pick)
        energies.append(jnp.asarray([place // moments for place in order], jnp.int32))
    table = mixing(branch_weight, pair_branch) / moments
    turned = couple_matrix.reshape(MODES, ORB, ORB, ATOMS_HERE).transpose(3, 0, 2, 1)
    turned = jnp.pad(turned, ((0, 0), (0, 0), (0, 6), (0, LANES - ORB))).reshape(-1, LANES)
    cols, rows = constants()
    weight, high, low = pl.pallas_call(
        prepare_kernel,
        in_specs=[smem, smem] + [vmem] * 8,
        out_specs=[vmem, vmem, vmem],
        out_shape=[
            pltpu.VMEM((ATOMS_HERE * MODES, DEPTH, 2 * LANES), bf16),
            pltpu.VMEM((2, MODES * POINTS, POINTS), bf16),
            pltpu.VMEM((2, MODES * POINTS, POINTS), bf16),
        ],
        compiler_params=PARAMS,
        cost_estimate=pl.CostEstimate(flops=10**9, bytes_accessed=4 * 10**6, transcendentals=0),
        name="prepare",
    )(
        occupation,
        energy_shift,
        turned,
        jnp.pad(table, ((0, 0), (0, 0), (0, LANES - moments))),
        cols,
        rows,
        jnp.asarray(np.pad(picks[0], ((0, 0), (0, LANES - moments)))),
        jnp.asarray(np.pad(picks[1].T, ((0, LANES - moments), (0, 0)))),
        energies[0][:, None],
        energies[1][None, :],
    )

    result = pl.pallas_call(
        compute_kernel,
        in_specs=[vmem] * 4,
        out_specs=vmem,
        out_shape=pltpu.VMEM((POINTS * ROWS, LANES), f32),
        compiler_params=PARAMS,
        name="compute",
    )(*(constrain(value, pltpu.VMEM) for value in (received, weight, high, low)))
    returned = exchange(result, back_order)
    out = pl.pallas_call(
        functools.partial(unpack_kernel, back_spots),
        in_specs=[vmem],
        out_specs=hbm,
        out_shape=pltpu.HBM((400, tiles * LANES), f32),
        scratch_shapes=[
            pltpu.VMEM((400, tiles * LANES), f32),
            pltpu.VMEM((LANES, LANES), f32),
            pltpu.SemaphoreType.DMA((9,)),
        ],
        compiler_params=PARAMS,
        name="unpack",
    )(constrain(returned, pltpu.VMEM))
    return out.reshape(green_blocks.shape)


def places(mesh, z_first):
    def key(place):
        energy, momentum = divmod(place, 8)
        chip = (2 * (momentum // 4) + (energy // 2) % 2, energy // 4, momentum % 4)
        return (energy % 2,) + (chip if z_first else chip[::-1])

    return sorted(range(mesh.size), key=key)


def solution(mesh):
    in_specs = (
        P(None, "energy", "momentum", None, None),
        P(None, None, ("energy", "momentum")),
        P(),
        P(),
        P(),
        P(),
    )
    out_specs = P(None, "energy", "momentum", None, None)
    orders = places(mesh, True), places(mesh, False)
    return jax.shard_map(
        functools.partial(on_device, *orders), mesh=mesh, in_specs=in_specs, out_specs=out_specs, check_vma=False
    )
```

```python
import functools

import jax
import jax.numpy as jnp
import numpy as np
from jax import lax
from jax.experimental import pallas as pl
from jax.experimental.pallas import tpu as pltpu
from jax.sharding import PartitionSpec as P

ORB = 10
PAIRS = ORB * ORB
DEPTH = 112
LANES = 128
ATOMS_HERE = 8
ROWS = 25
POINTS = 128
MODES = 3
AXES = ("energy", "momentum")
HIGHEST = lax.Precision.HIGHEST
constrain = pltpu.with_memory_space_constraint
PARAMS = pltpu.CompilerParams(vmem_limit_bytes=32 * 1024 * 1024)


def split(value):
    high = value.astype(jnp.bfloat16)
    low = (value - high.astype(jnp.float32)).astype(jnp.bfloat16)
    return high, low


def dot(left, right):
    return lax.dot(left, right, preferred_element_type=jnp.float32)


def turn(value, lanes):
    return pltpu.roll(value, lanes % LANES, 1) if lanes % LANES else value


def pack_kernel(spots, green_ref, out_ref, held_ref, message_ref, rest_ref, sems, out_sems):
    rest_copy = pltpu.make_async_copy(
        green_ref.at[pl.ds(384, 16), :], held_ref.at[pl.ds(384, 16), :], sems.at[2]
    )
    rest_copy.start()
    copies = []
    for part in range(2):
        place = (pl.ds(0, 384), pl.ds(512 * part, 512))
        copies.append(
            pltpu.make_async_copy(green_ref.at[place], held_ref.at[place], sems.at[part])
        )
        copies[part].start()
    rest_copy.wait()
    rest_ref[...] = jnp.concatenate(
        [held_ref[384:400, LANES * g : LANES * (g + 1)] for g in range(8)], axis=0
    ).T
    lane = lax.broadcasted_iota(jnp.int32, (16, LANES), 1)
    pieces = [rest_ref[pl.ds(atom, 16, stride=8), :] for atom in range(8)]
    for group in range(8):
        joined = None
        for atom in range(8):
            piece = turn(pieces[atom], 16 * (atom - group))
            joined = piece if joined is None else jnp.where(lane < 16 * atom, joined, piece)
        for first in range(0, 16, 4):
            row = ROWS * spots[16 * group + first] + 24
            step = ROWS * (spots[1] - spots[0])
            message_ref[pl.ds(row, 4, stride=step), :] = joined[first : first + 4, :]
    waited, filled, sent = set(), [0] * 8, []
    for group in (0, 2, 4, 6, 1, 3, 5, 7):
        if group // 4 not in waited:
            copies[group // 4].wait()
            waited.add(group // 4)
        for tile in range(3):
            turned = held_ref[
                LANES * tile : LANES * (tile + 1), LANES * group : LANES * (group + 1)
            ].T
            for owner in range(16):
                row = ROWS * spots[16 * group + owner] + 8 * tile
                message_ref[row : row + 8, :] = turned[8 * owner : 8 * owner + 8, :]
        for owner in range(16):
            block = spots[16 * group + owner] // 16
            filled[block] += 1
            if filled[block] == 16:
                place = pl.ds(400 * block, 400)
                sent.append(
                    pltpu.make_async_copy(
                        message_ref.at[place], out_ref.at[place], out_sems.at[block]
                    )
                )
                sent[-1].start()
    for copy in sent:
        copy.wait()


def unpack_kernel(spots, in_ref, out_ref, held_ref, rest_ref, sems):
    lane = lax.broadcasted_iota(jnp.int32, (16, LANES), 1)
    pieces = []
    for group in range(8):
        rows = [ROWS * spots[16 * group + first] + 24 for first in range(0, 16, 4)]
        step = ROWS * (spots[1] - spots[0])
        pieces.append(
            jnp.concatenate([in_ref[pl.ds(row, 4, stride=step), :] for row in rows], axis=0)
        )
    for atom in range(8):
        joined = None
        for group in range(8):
            piece = turn(pieces[group], 16 * (group - atom))
            joined = piece if joined is None else jnp.where(lane < 16 * group, joined, piece)
        rest_ref[pl.ds(atom, 16, stride=8), :] = joined
    turned = rest_ref[...].T
    for group in range(8):
        held_ref[384:400, LANES * group : LANES * (group + 1)] = turned[
            16 * group : 16 * group + 16, :
        ]
    copies = [
        pltpu.make_async_copy(
            held_ref.at[pl.ds(384, 16), :], out_ref.at[pl.ds(384, 16), :], sems.at[8]
        )
    ]
    copies[0].start()
    for group in range(8):
        for tile in range(3):
            rows = [ROWS * spots[16 * group + owner] + 8 * tile for owner in range(16)]
            held_ref[
                LANES * tile : LANES * (tile + 1), LANES * group : LANES * (group + 1)
            ] = jnp.concatenate([in_ref[row : row + 8, :] for row in rows], axis=0).T
        place = (pl.ds(0, 384), pl.ds(LANES * group, LANES))
        copies.append(
            pltpu.make_async_copy(held_ref.at[place], out_ref.at[place], sems.at[group])
        )
        copies[-1].start()
    for copy in copies:
        copy.wait()


def prepare_kernel(
    occ_ref,
    shift_ref,
    couple_ref,
    mix_ref,
    cols_ref,
    rows_ref,
    pick_ref,
    picked_ref,
    row_ref,
    col_ref,
    out_ref,
    high_ref,
    low_ref,
):
    spread = lax.dot(
        couple_ref[...], cols_ref[...], precision=HIGHEST, preferred_element_type=jnp.float32
    )
    for index in range(ATOMS_HERE * MODES):
        part = spread[16 * index : 16 * index + 16, :]
        first = lax.dot(
            rows_ref[:LANES, :], part[:, :LANES], precision=HIGHEST,
            preferred_element_type=jnp.float32,
        )
        second = lax.dot(
            rows_ref[LANES:, :], part[:, LANES:], precision=HIGHEST,
            preferred_element_type=jnp.float32,
        )
        high, low = split(first * second)
        out_ref[index, :, :LANES] = high[:DEPTH]
        out_ref[index, :, LANES:] = low[:DEPTH]
    row = jnp.broadcast_to(row_ref[...], (POINTS, POINTS))
    col = jnp.broadcast_to(col_ref[...], (POINTS, POINTS))
    for mode in range(MODES):
        step = shift_ref[mode]
        above = col == row + step
        below = col == row - step
        mixing = lax.dot(
            lax.dot(
                pick_ref[:, :8], mix_ref[mode], precision=HIGHEST,
                preferred_element_type=jnp.float32,
            ),
            picked_ref[...], precision=HIGHEST, preferred_element_type=jnp.float32,
        )
        for kind in range(2):
            upper = occ_ref[mode] + (1.0 - kind)
            lower = occ_ref[mode] + float(kind)
            moved = jnp.where(above, upper, 0.0) + jnp.where(below, lower, 0.0)
            high, low = split(moved * mixing)
            high_ref[kind, POINTS * mode : POINTS * (mode + 1), :] = high
            low_ref[kind, POINTS * mode : POINTS * (mode + 1), :] = low


def compute_kernel(x_ref, weight_ref, high_ref, low_ref, out_ref):
    lane = lax.broadcasted_iota(jnp.int32, (POINTS, LANES), 1)
    rest = x_ref[pl.ds(24, POINTS, stride=ROWS), :]
    blank = jnp.zeros((LANES - DEPTH, 2 * LANES), jnp.bfloat16)

    def shifted(atom):
        tiles = [x_ref[pl.ds(8 * t + atom, POINTS, stride=ROWS), :] for t in range(3)]
        tiles.append(turn(rest, -16 * atom))
        blocks = [tiles[0]]
        for b in range(1, 4):
            joined = jnp.where(lane < PAIRS - 28 * b, tiles[b], tiles[b - 1])
            blocks.append(turn(joined, 28 * b))
        parts = []
        for kind in range(2):
            x_high, x_low = split(jnp.concatenate(blocks[2 * kind : 2 * kind + 2], axis=1))
            table = high_ref[kind]
            moved = dot(
                jnp.concatenate([table, table], axis=1), jnp.concatenate([x_high, x_low], axis=0)
            ) + dot(low_ref[kind], x_high)
            parts.append(split(moved))
        return parts

    def sandwiched(atom, parts):
        rows = []
        for high, low in parts:
            for part in range(2):
                lanes = slice(LANES * part, LANES * (part + 1))
                pieces = []
                for mode in range(MODES):
                    points = slice(POINTS * mode, POINTS * (mode + 1))
                    pieces += [high[points, lanes], low[points, lanes]]
                rows.append(jnp.concatenate(pieces, axis=1))
        weights = []
        for mode in range(MODES):
            both = jnp.concatenate([weight_ref[MODES * atom + mode], blank], axis=0)
            weights += [
                both,
                jnp.concatenate([both[:, :LANES], jnp.zeros_like(both[:, LANES:])], axis=1),
            ]
        result = dot(jnp.concatenate(rows, axis=0), jnp.concatenate(weights, axis=0))
        return result[:, :LANES] + result[:, LANES:]

    rest_out = jnp.zeros((POINTS, LANES), jnp.float32)
    parts = shifted(0)
    for atom in range(ATOMS_HERE):
        following = shifted(atom + 1) if atom + 1 < ATOMS_HERE else None
        result = sandwiched(atom, parts)
        turned = [turn(result[POINTS * b : POINTS * (b + 1)], -28 * b) for b in range(4)]
        for t in range(3):
            out_ref[pl.ds(8 * t + atom, POINTS, stride=ROWS), :] = jnp.where(
                lane < PAIRS - 28 * t, turned[t], turned[t + 1]
            )
        rest_out = rest_out + turn(jnp.where(lane < 16, turned[3], 0.0), 16 * atom)
        parts = following
    out_ref[pl.ds(24, POINTS, stride=ROWS), :] = rest_out


def constants():
    pair = np.arange(LANES)
    valid = pair < PAIRS
    cols = np.zeros((LANES, 2 * LANES), np.float32)
    rows = np.zeros((2 * LANES, 16), np.float32)
    for k in range(ORB):
        cols[k, :LANES] = valid & (pair // ORB == k)
        cols[k, LANES:] = valid & (pair % ORB == k)
        rows[:LANES, k] = valid & (pair // ORB == k)
        rows[LANES:, k] = valid & (pair % ORB == k)
    return jnp.asarray(cols), jnp.asarray(rows)


def exchange(message, order):
    moved = lax.all_to_all(
        message.reshape(POINTS, ROWS, 1, LANES),
        AXES,
        split_axis=0,
        concat_axis=0,
        tiled=True,
        axis_index_groups=[order],
    )
    return moved.reshape(POINTS * ROWS, LANES)


def mixing(branch_weight, pair_branch):
    onehot = (
        pair_branch[:, :, None] == jnp.arange(branch_weight.shape[0], dtype=jnp.int32)
    ).astype(jnp.float32)
    return jnp.einsum("kjq,qm->mkj", onehot, branch_weight, precision=HIGHEST)


def on_device(
    out_order, back_order, green_blocks, couple_matrix, occupation, energy_shift, branch_weight, pair_branch
):
    f32, bf16 = jnp.float32, jnp.bfloat16
    out_spots = [out_order.index(device) for device in range(POINTS)]
    back_spots = [back_order.index(device) for device in range(POINTS)]
    smem = pl.BlockSpec(memory_space=pltpu.SMEM)
    vmem = pl.BlockSpec(memory_space=pltpu.VMEM)
    hbm = pl.BlockSpec(memory_space=pltpu.HBM)
    tiles = green_blocks.shape[4] // LANES
    message = pl.pallas_call(
        functools.partial(pack_kernel, out_spots),
        in_specs=[hbm],
        out_specs=hbm,
        out_shape=pltpu.HBM((POINTS * ROWS, LANES), f32),
        scratch_shapes=[
            pltpu.VMEM((400, tiles * LANES), f32),
            pltpu.VMEM((POINTS * ROWS, LANES), f32),
            pltpu.VMEM((LANES, LANES), f32),
            pltpu.SemaphoreType.DMA((3,)),
            pltpu.SemaphoreType.DMA((8,)),
        ],
        compiler_params=PARAMS,
        name="pack",
    )(constrain(green_blocks.reshape(400, tiles * LANES), pltpu.HBM))
    received = exchange(message, out_order)

    moments = pair_branch.shape[0]
    picks, energies = [], []
    for order in (back_order, out_order):
        pick = np.zeros((POINTS, moments), np.float32)
        pick[np.arange(POINTS), [place % moments for place in order]] = 1.0
        picks.append(pick)
        energies.append(jnp.asarray([place // moments for place in order], jnp.int32))
    table = mixing(branch_weight, pair_branch) / moments
    turned = couple_matrix.reshape(MODES, ORB, ORB, ATOMS_HERE).transpose(3, 0, 2, 1)
    turned = jnp.pad(turned, ((0, 0), (0, 0), (0, 6), (0, LANES - ORB))).reshape(-1, LANES)
    cols, rows = constants()
    weight, high, low = pl.pallas_call(
        prepare_kernel,
        in_specs=[smem, smem] + [vmem] * 8,
        out_specs=[vmem, vmem, vmem],
        out_shape=[
            pltpu.VMEM((ATOMS_HERE * MODES, DEPTH, 2 * LANES), bf16),
            pltpu.VMEM((2, MODES * POINTS, POINTS), bf16),
            pltpu.VMEM((2, MODES * POINTS, POINTS), bf16),
        ],
        compiler_params=PARAMS,
        cost_estimate=pl.CostEstimate(flops=10**9, bytes_accessed=4 * 10**6, transcendentals=0),
        name="prepare",
    )(
        occupation,
        energy_shift,
        turned,
        jnp.pad(table, ((0, 0), (0, 0), (0, LANES - moments))),
        cols,
        rows,
        jnp.asarray(np.pad(picks[0], ((0, 0), (0, LANES - moments)))),
        jnp.asarray(np.pad(picks[1].T, ((0, LANES - moments), (0, 0)))),
        energies[0][:, None],
        energies[1][None, :],
    )

    result = pl.pallas_call(
        compute_kernel,
        in_specs=[vmem] * 4,
        out_specs=vmem,
        out_shape=pltpu.VMEM((POINTS * ROWS, LANES), f32),
        compiler_params=PARAMS,
        name="compute",
    )(*(constrain(value, pltpu.VMEM) for value in (received, weight, high, low)))
    returned = exchange(result, back_order)
    out = pl.pallas_call(
        functools.partial(unpack_kernel, back_spots),
        in_specs=[vmem],
        out_specs=hbm,
        out_shape=pltpu.HBM((400, tiles * LANES), f32),
        scratch_shapes=[
            pltpu.VMEM((400, tiles * LANES), f32),
            pltpu.VMEM((LANES, LANES), f32),
            pltpu.SemaphoreType.DMA((9,)),
        ],
        compiler_params=PARAMS,
        name="unpack",
    )(constrain(returned, pltpu.VMEM))
    return out.reshape(green_blocks.shape)


def places(mesh, z_first):
    def key(place):
        energy, momentum = divmod(place, 8)
        x, y, z = momentum % 4, energy // 4, 2 * (momentum // 4) + (energy // 2) % 2
        return (energy % 2,) + ((z, x, y) if z_first else (x, y, z))

    return sorted(range(mesh.size), key=key)


def solution(mesh):
    in_specs = (
        P(None, "energy", "momentum", None, None),
        P(None, None, ("energy", "momentum")),
        P(),
        P(),
        P(),
        P(),
    )
    out_specs = P(None, "energy", "momentum", None, None)
    orders = places(mesh, True), places(mesh, False)
    return jax.shard_map(
        functools.partial(on_device, *orders), mesh=mesh, in_specs=in_specs, out_specs=out_specs, check_vma=False
    )
```

```python
import functools

import jax
import jax.numpy as jnp
import numpy as np
from jax import lax
from jax.experimental import pallas as pl
from jax.experimental.pallas import tpu as pltpu
from jax.sharding import PartitionSpec as P

ORB = 10
PAIRS = ORB * ORB
DEPTH = 112
LANES = 128
ATOMS_HERE = 8
ROWS = 25
POINTS = 128
MODES = 3
AXES = ("energy", "momentum")
HIGHEST = lax.Precision.HIGHEST
constrain = pltpu.with_memory_space_constraint
PARAMS = pltpu.CompilerParams(vmem_limit_bytes=32 * 1024 * 1024)


def split(value):
    high = value.astype(jnp.bfloat16)
    low = (value - high.astype(jnp.float32)).astype(jnp.bfloat16)
    return high, low


def dot(left, right):
    return lax.dot(left, right, preferred_element_type=jnp.float32)


def turn(value, lanes):
    return pltpu.roll(value, lanes % LANES, 1) if lanes % LANES else value


def pack_kernel(spots, green_ref, out_ref, held_ref, message_ref, rest_ref, sems, out_sems):
    rest_copy = pltpu.make_async_copy(
        green_ref.at[pl.ds(384, 16), :], held_ref.at[pl.ds(384, 16), :], sems.at[2]
    )
    rest_copy.start()
    copies = []
    for part in range(2):
        place = (pl.ds(0, 384), pl.ds(512 * part, 512))
        copies.append(
            pltpu.make_async_copy(green_ref.at[place], held_ref.at[place], sems.at[part])
        )
        copies[part].start()
    rest_copy.wait()
    rest_ref[...] = jnp.concatenate(
        [held_ref[384:400, LANES * g : LANES * (g + 1)] for g in range(8)], axis=0
    ).T
    lane = lax.broadcasted_iota(jnp.int32, (16, LANES), 1)
    pieces = [rest_ref[pl.ds(atom, 16, stride=8), :] for atom in range(8)]
    for group in range(8):
        joined = None
        for atom in range(8):
            piece = turn(pieces[atom], 16 * (atom - group))
            joined = piece if joined is None else jnp.where(lane < 16 * atom, joined, piece)
        for first in range(0, 16, 4):
            row = ROWS * spots[16 * group + first] + 24
            step = ROWS * (spots[1] - spots[0])
            message_ref[pl.ds(row, 4, stride=step), :] = joined[first : first + 4, :]
    waited, filled, sent = set(), [0] * 8, []
    for group in range(8):
        if group // 4 not in waited:
            copies[group // 4].wait()
            waited.add(group // 4)
        for tile in range(3):
            turned = held_ref[
                LANES * tile : LANES * (tile + 1), LANES * group : LANES * (group + 1)
            ].T
            for owner in range(16):
                row = ROWS * spots[16 * group + owner] + 8 * tile
                message_ref[row : row + 8, :] = turned[8 * owner : 8 * owner + 8, :]
        for owner in range(16):
            block = spots[16 * group + owner] // 16
            filled[block] += 1
            if filled[block] == 16:
                place = pl.ds(400 * block, 400)
                sent.append(
                    pltpu.make_async_copy(
                        message_ref.at[place], out_ref.at[place], out_sems.at[block]
                    )
                )
                sent[-1].start()
    for copy in sent:
        copy.wait()


def unpack_kernel(spots, in_ref, out_ref, held_ref, rest_ref, sems):
    lane = lax.broadcasted_iota(jnp.int32, (16, LANES), 1)
    pieces = []
    for group in range(8):
        rows = [ROWS * spots[16 * group + first] + 24 for first in range(0, 16, 4)]
        step = ROWS * (spots[1] - spots[0])
        pieces.append(
            jnp.concatenate([in_ref[pl.ds(row, 4, stride=step), :] for row in rows], axis=0)
        )
    for atom in range(8):
        joined = None
        for group in range(8):
            piece = turn(pieces[group], 16 * (group - atom))
            joined = piece if joined is None else jnp.where(lane < 16 * group, joined, piece)
        rest_ref[pl.ds(atom, 16, stride=8), :] = joined
    turned = rest_ref[...].T
    for group in range(8):
        held_ref[384:400, LANES * group : LANES * (group + 1)] = turned[
            16 * group : 16 * group + 16, :
        ]
    copies = [
        pltpu.make_async_copy(
            held_ref.at[pl.ds(384, 16), :], out_ref.at[pl.ds(384, 16), :], sems.at[8]
        )
    ]
    copies[0].start()
    for group in range(8):
        for tile in range(3):
            rows = [ROWS * spots[16 * group + owner] + 8 * tile for owner in range(16)]
            held_ref[
                LANES * tile : LANES * (tile + 1), LANES * group : LANES * (group + 1)
            ] = jnp.concatenate([in_ref[row : row + 8, :] for row in rows], axis=0).T
        place = (pl.ds(0, 384), pl.ds(LANES * group, LANES))
        copies.append(
            pltpu.make_async_copy(held_ref.at[place], out_ref.at[place], sems.at[group])
        )
        copies[-1].start()
    for copy in copies:
        copy.wait()


def prepare_kernel(
    occ_ref,
    shift_ref,
    couple_ref,
    mix_ref,
    cols_ref,
    rows_ref,
    pick_ref,
    picked_ref,
    row_ref,
    col_ref,
    out_ref,
    high_ref,
    low_ref,
):
    spread = lax.dot(
        couple_ref[...], cols_ref[...], precision=HIGHEST, preferred_element_type=jnp.float32
    )
    for index in range(ATOMS_HERE * MODES):
        part = spread[16 * index : 16 * index + 16, :]
        first = lax.dot(
            rows_ref[:LANES, :], part[:, :LANES], precision=HIGHEST,
            preferred_element_type=jnp.float32,
        )
        second = lax.dot(
            rows_ref[LANES:, :], part[:, LANES:], precision=HIGHEST,
            preferred_element_type=jnp.float32,
        )
        high, low = split(first * second)
        out_ref[index, :, :LANES] = high[:DEPTH]
        out_ref[index, :, LANES:] = low[:DEPTH]
    row = jnp.broadcast_to(row_ref[...], (POINTS, POINTS))
    col = jnp.broadcast_to(col_ref[...], (POINTS, POINTS))
    for mode in range(MODES):
        step = shift_ref[mode]
        above = col == row + step
        below = col == row - step
        mixing = lax.dot(
            lax.dot(
                pick_ref[:, :8], mix_ref[mode], precision=HIGHEST,
                preferred_element_type=jnp.float32,
            ),
            picked_ref[...], precision=HIGHEST, preferred_element_type=jnp.float32,
        )
        for kind in range(2):
            upper = occ_ref[mode] + (1.0 - kind)
            lower = occ_ref[mode] + float(kind)
            moved = jnp.where(above, upper, 0.0) + jnp.where(below, lower, 0.0)
            high, low = split(moved * mixing)
            high_ref[kind, POINTS * mode : POINTS * (mode + 1), :] = high
            low_ref[kind, POINTS * mode : POINTS * (mode + 1), :] = low


def compute_kernel(x_ref, weight_ref, high_ref, low_ref, out_ref):
    lane = lax.broadcasted_iota(jnp.int32, (POINTS, LANES), 1)
    rest = x_ref[pl.ds(24, POINTS, stride=ROWS), :]
    blank = jnp.zeros((LANES - DEPTH, 2 * LANES), jnp.bfloat16)

    def shifted(atom):
        tiles = [x_ref[pl.ds(8 * t + atom, POINTS, stride=ROWS), :] for t in range(3)]
        tiles.append(turn(rest, -16 * atom))
        blocks = [tiles[0]]
        for b in range(1, 4):
            joined = jnp.where(lane < PAIRS - 28 * b, tiles[b], tiles[b - 1])
            blocks.append(turn(joined, 28 * b))
        parts = []
        for kind in range(2):
            x_high, x_low = split(jnp.concatenate(blocks[2 * kind : 2 * kind + 2], axis=1))
            table = high_ref[kind]
            moved = dot(
                jnp.concatenate([table, table], axis=1), jnp.concatenate([x_high, x_low], axis=0)
            ) + dot(low_ref[kind], x_high)
            parts.append(split(moved))
        return parts

    def sandwiched(atom, parts):
        rows = []
        for high, low in parts:
            for part in range(2):
                lanes = slice(LANES * part, LANES * (part + 1))
                pieces = []
                for mode in range(MODES):
                    points = slice(POINTS * mode, POINTS * (mode + 1))
                    pieces += [high[points, lanes], low[points, lanes]]
                rows.append(jnp.concatenate(pieces, axis=1))
        weights = []
        for mode in range(MODES):
            both = jnp.concatenate([weight_ref[MODES * atom + mode], blank], axis=0)
            weights += [
                both,
                jnp.concatenate([both[:, :LANES], jnp.zeros_like(both[:, LANES:])], axis=1),
            ]
        result = dot(jnp.concatenate(rows, axis=0), jnp.concatenate(weights, axis=0))
        return result[:, :LANES] + result[:, LANES:]

    rest_out = jnp.zeros((POINTS, LANES), jnp.float32)
    parts = shifted(0)
    for atom in range(ATOMS_HERE):
        following = shifted(atom + 1) if atom + 1 < ATOMS_HERE else None
        result = sandwiched(atom, parts)
        turned = [turn(result[POINTS * b : POINTS * (b + 1)], -28 * b) for b in range(4)]
        for t in range(3):
            out_ref[pl.ds(8 * t + atom, POINTS, stride=ROWS), :] = jnp.where(
                lane < PAIRS - 28 * t, turned[t], turned[t + 1]
            )
        rest_out = rest_out + turn(jnp.where(lane < 16, turned[3], 0.0), 16 * atom)
        parts = following
    out_ref[pl.ds(24, POINTS, stride=ROWS), :] = rest_out


def constants():
    pair = np.arange(LANES)
    valid = pair < PAIRS
    cols = np.zeros((LANES, 2 * LANES), np.float32)
    rows = np.zeros((2 * LANES, 16), np.float32)
    for k in range(ORB):
        cols[k, :LANES] = valid & (pair // ORB == k)
        cols[k, LANES:] = valid & (pair % ORB == k)
        rows[:LANES, k] = valid & (pair // ORB == k)
        rows[LANES:, k] = valid & (pair % ORB == k)
    return jnp.asarray(cols), jnp.asarray(rows)


def exchange(message, order):
    moved = lax.all_to_all(
        message.reshape(POINTS, ROWS, 1, LANES),
        AXES,
        split_axis=0,
        concat_axis=0,
        tiled=True,
        axis_index_groups=[order],
    )
    return moved.reshape(POINTS * ROWS, LANES)


def mixing(branch_weight, pair_branch):
    onehot = (
        pair_branch[:, :, None] == jnp.arange(branch_weight.shape[0], dtype=jnp.int32)
    ).astype(jnp.float32)
    return jnp.einsum("kjq,qm->mkj", onehot, branch_weight, precision=HIGHEST)


def on_device(
    out_order, back_order, green_blocks, couple_matrix, occupation, energy_shift, branch_weight, pair_branch
):
    f32, bf16 = jnp.float32, jnp.bfloat16
    out_spots = [out_order.index(device) for device in range(POINTS)]
    back_spots = [back_order.index(device) for device in range(POINTS)]
    smem = pl.BlockSpec(memory_space=pltpu.SMEM)
    vmem = pl.BlockSpec(memory_space=pltpu.VMEM)
    hbm = pl.BlockSpec(memory_space=pltpu.HBM)
    tiles = green_blocks.shape[4] // LANES
    message = pl.pallas_call(
        functools.partial(pack_kernel, out_spots),
        in_specs=[hbm],
        out_specs=hbm,
        out_shape=pltpu.HBM((POINTS * ROWS, LANES), f32),
        scratch_shapes=[
            pltpu.VMEM((400, tiles * LANES), f32),
            pltpu.VMEM((POINTS * ROWS, LANES), f32),
            pltpu.VMEM((LANES, LANES), f32),
            pltpu.SemaphoreType.DMA((3,)),
            pltpu.SemaphoreType.DMA((8,)),
        ],
        compiler_params=PARAMS,
        name="pack",
    )(constrain(green_blocks.reshape(400, tiles * LANES), pltpu.HBM))
    received = exchange(message, out_order)

    moments = pair_branch.shape[0]
    picks, energies = [], []
    for order in (back_order, out_order):
        pick = np.zeros((POINTS, moments), np.float32)
        pick[np.arange(POINTS), [place % moments for place in order]] = 1.0
        picks.append(pick)
        energies.append(jnp.asarray([place // moments for place in order], jnp.int32))
    table = mixing(branch_weight, pair_branch) / moments
    turned = couple_matrix.reshape(MODES, ORB, ORB, ATOMS_HERE).transpose(3, 0, 2, 1)
    turned = jnp.pad(turned, ((0, 0), (0, 0), (0, 6), (0, LANES - ORB))).reshape(-1, LANES)
    cols, rows = constants()
    weight, high, low = pl.pallas_call(
        prepare_kernel,
        in_specs=[smem, smem] + [vmem] * 8,
        out_specs=[vmem, vmem, vmem],
        out_shape=[
            pltpu.VMEM((ATOMS_HERE * MODES, DEPTH, 2 * LANES), bf16),
            pltpu.VMEM((2, MODES * POINTS, POINTS), bf16),
            pltpu.VMEM((2, MODES * POINTS, POINTS), bf16),
        ],
        compiler_params=PARAMS,
        cost_estimate=pl.CostEstimate(flops=10**9, bytes_accessed=4 * 10**6, transcendentals=0),
        name="prepare",
    )(
        occupation,
        energy_shift,
        turned,
        jnp.pad(table, ((0, 0), (0, 0), (0, LANES - moments))),
        cols,
        rows,
        jnp.asarray(np.pad(picks[0], ((0, 0), (0, LANES - moments)))),
        jnp.asarray(np.pad(picks[1].T, ((0, LANES - moments), (0, 0)))),
        energies[0][:, None],
        energies[1][None, :],
    )

    result = pl.pallas_call(
        compute_kernel,
        in_specs=[vmem] * 4,
        out_specs=vmem,
        out_shape=pltpu.VMEM((POINTS * ROWS, LANES), f32),
        compiler_params=PARAMS,
        name="compute",
    )(*(constrain(value, pltpu.VMEM) for value in (received, weight, high, low)))
    returned = exchange(result, back_order)
    out = pl.pallas_call(
        functools.partial(unpack_kernel, back_spots),
        in_specs=[vmem],
        out_specs=hbm,
        out_shape=pltpu.HBM((400, tiles * LANES), f32),
        scratch_shapes=[
            pltpu.VMEM((400, tiles * LANES), f32),
            pltpu.VMEM((LANES, LANES), f32),
            pltpu.SemaphoreType.DMA((9,)),
        ],
        compiler_params=PARAMS,
        name="unpack",
    )(constrain(returned, pltpu.VMEM))
    return out.reshape(green_blocks.shape)


def places(mesh, y_first):
    def key(place):
        energy, momentum = divmod(place, 8)
        x, y, z = momentum % 4, energy // 4, 2 * (momentum // 4) + (energy // 2) % 2
        return (energy % 2,) + ((y, z, x) if y_first else (x, y, z))

    return sorted(range(mesh.size), key=key)


def solution(mesh):
    in_specs = (
        P(None, "energy", "momentum", None, None),
        P(None, None, ("energy", "momentum")),
        P(),
        P(),
        P(),
        P(),
    )
    out_specs = P(None, "energy", "momentum", None, None)
    orders = places(mesh, True), places(mesh, False)
    return jax.shard_map(
        functools.partial(on_device, *orders), mesh=mesh, in_specs=in_specs, out_specs=out_specs, check_vma=False
    )
```

```python
import functools

import jax
import jax.numpy as jnp
import numpy as np
from jax import lax
from jax.experimental import pallas as pl
from jax.experimental.pallas import tpu as pltpu
from jax.sharding import PartitionSpec as P

ORB = 10
PAIRS = ORB * ORB
DEPTH = 112
LANES = 128
ATOMS_HERE = 8
ROWS = 25
POINTS = 128
MODES = 3
AXES = ("energy", "momentum")
HIGHEST = lax.Precision.HIGHEST
constrain = pltpu.with_memory_space_constraint
PARAMS = pltpu.CompilerParams(vmem_limit_bytes=32 * 1024 * 1024)


def split(value):
    high = value.astype(jnp.bfloat16)
    low = (value - high.astype(jnp.float32)).astype(jnp.bfloat16)
    return high, low


def dot(left, right):
    return lax.dot(left, right, preferred_element_type=jnp.float32)


def turn(value, lanes):
    return pltpu.roll(value, lanes % LANES, 1) if lanes % LANES else value


def pack_kernel(spots, green_ref, out_ref, held_ref, message_ref, rest_ref, sems, out_sems):
    rest_copy = pltpu.make_async_copy(
        green_ref.at[pl.ds(384, 16), :], held_ref.at[pl.ds(384, 16), :], sems.at[2]
    )
    rest_copy.start()
    copies = []
    for part in range(2):
        place = (pl.ds(0, 384), pl.ds(512 * part, 512))
        copies.append(
            pltpu.make_async_copy(green_ref.at[place], held_ref.at[place], sems.at[part])
        )
        copies[part].start()
    rest_copy.wait()
    rest_ref[...] = jnp.concatenate(
        [held_ref[384:400, LANES * g : LANES * (g + 1)] for g in range(8)], axis=0
    ).T
    lane = lax.broadcasted_iota(jnp.int32, (16, LANES), 1)
    pieces = [rest_ref[pl.ds(atom, 16, stride=8), :] for atom in range(8)]
    for group in range(8):
        joined = None
        for atom in range(8):
            piece = turn(pieces[atom], 16 * (atom - group))
            joined = piece if joined is None else jnp.where(lane < 16 * atom, joined, piece)
        for first in range(0, 16, 4):
            row = ROWS * spots[16 * group + first] + 24
            step = ROWS * (spots[1] - spots[0])
            message_ref[pl.ds(row, 4, stride=step), :] = joined[first : first + 4, :]
    waited, filled, sent = set(), [0] * 8, []
    for group in range(8):
        if group // 4 not in waited:
            copies[group // 4].wait()
            waited.add(group // 4)
        for tile in range(3):
            turned = held_ref[
                LANES * tile : LANES * (tile + 1), LANES * group : LANES * (group + 1)
            ].T
            for owner in range(16):
                row = ROWS * spots[16 * group + owner] + 8 * tile
                message_ref[row : row + 8, :] = turned[8 * owner : 8 * owner + 8, :]
        for owner in range(16):
            block = spots[16 * group + owner] // 16
            filled[block] += 1
            if filled[block] == 16:
                place = pl.ds(400 * block, 400)
                sent.append(
                    pltpu.make_async_copy(
                        message_ref.at[place], out_ref.at[place], out_sems.at[block]
                    )
                )
                sent[-1].start()
    for copy in sent:
        copy.wait()


def unpack_kernel(spots, in_ref, out_ref, held_ref, rest_ref, sems):
    copies = []
    for group in range(8):
        for tile in range(3):
            rows = [ROWS * spots[16 * group + owner] + 8 * tile for owner in range(16)]
            held_ref[
                LANES * tile : LANES * (tile + 1), LANES * group : LANES * (group + 1)
            ] = jnp.concatenate([in_ref[row : row + 8, :] for row in rows], axis=0).T
        place = (pl.ds(0, 384), pl.ds(LANES * group, LANES))
        copies.append(
            pltpu.make_async_copy(held_ref.at[place], out_ref.at[place], sems.at[group])
        )
        copies[-1].start()
    lane = lax.broadcasted_iota(jnp.int32, (16, LANES), 1)
    pieces = []
    for group in range(8):
        rows = [ROWS * spots[16 * group + first] + 24 for first in range(0, 16, 4)]
        step = ROWS * (spots[1] - spots[0])
        pieces.append(
            jnp.concatenate([in_ref[pl.ds(row, 4, stride=step), :] for row in rows], axis=0)
        )
    for atom in range(8):
        joined = None
        for group in range(8):
            piece = turn(pieces[group], 16 * (group - atom))
            joined = piece if joined is None else jnp.where(lane < 16 * group, joined, piece)
        rest_ref[pl.ds(atom, 16, stride=8), :] = joined
    turned = rest_ref[...].T
    for group in range(8):
        held_ref[384:400, LANES * group : LANES * (group + 1)] = turned[
            16 * group : 16 * group + 16, :
        ]
    copies.append(
        pltpu.make_async_copy(
            held_ref.at[pl.ds(384, 16), :], out_ref.at[pl.ds(384, 16), :], sems.at[8]
        )
    )
    copies[-1].start()
    for copy in copies:
        copy.wait()


def prepare_kernel(
    occ_ref,
    shift_ref,
    couple_ref,
    mix_ref,
    cols_ref,
    rows_ref,
    pick_ref,
    picked_ref,
    row_ref,
    col_ref,
    out_ref,
    high_ref,
    low_ref,
):
    spread = lax.dot(
        couple_ref[...], cols_ref[...], precision=HIGHEST, preferred_element_type=jnp.float32
    )
    for index in range(ATOMS_HERE * MODES):
        part = spread[16 * index : 16 * index + 16, :]
        first = lax.dot(
            rows_ref[:LANES, :], part[:, :LANES], precision=HIGHEST,
            preferred_element_type=jnp.float32,
        )
        second = lax.dot(
            rows_ref[LANES:, :], part[:, LANES:], precision=HIGHEST,
            preferred_element_type=jnp.float32,
        )
        high, low = split(first * second)
        out_ref[index, :, :LANES] = high[:DEPTH]
        out_ref[index, :, LANES:] = low[:DEPTH]
    row = jnp.broadcast_to(row_ref[...], (POINTS, POINTS))
    col = jnp.broadcast_to(col_ref[...], (POINTS, POINTS))
    for mode in range(MODES):
        step = shift_ref[mode]
        above = col == row + step
        below = col == row - step
        mixing = lax.dot(
            lax.dot(
                pick_ref[:, :8], mix_ref[mode], precision=HIGHEST,
                preferred_element_type=jnp.float32,
            ),
            picked_ref[...], precision=HIGHEST, preferred_element_type=jnp.float32,
        )
        for kind in range(2):
            upper = occ_ref[mode] + (1.0 - kind)
            lower = occ_ref[mode] + float(kind)
            moved = jnp.where(above, upper, 0.0) + jnp.where(below, lower, 0.0)
            high, low = split(moved * mixing)
            high_ref[kind, POINTS * mode : POINTS * (mode + 1), :] = high
            low_ref[kind, POINTS * mode : POINTS * (mode + 1), :] = low


def compute_kernel(x_ref, weight_ref, high_ref, low_ref, out_ref):
    lane = lax.broadcasted_iota(jnp.int32, (POINTS, LANES), 1)
    rest = x_ref[pl.ds(24, POINTS, stride=ROWS), :]
    blank = jnp.zeros((LANES - DEPTH, 2 * LANES), jnp.bfloat16)

    def shifted(atom):
        tiles = [x_ref[pl.ds(8 * t + atom, POINTS, stride=ROWS), :] for t in range(3)]
        tiles.append(turn(rest, -16 * atom))
        blocks = [tiles[0]]
        for b in range(1, 4):
            joined = jnp.where(lane < PAIRS - 28 * b, tiles[b], tiles[b - 1])
            blocks.append(turn(joined, 28 * b))
        parts = []
        for kind in range(2):
            x_high, x_low = split(jnp.concatenate(blocks[2 * kind : 2 * kind + 2], axis=1))
            table = high_ref[kind]
            moved = dot(
                jnp.concatenate([table, table], axis=1), jnp.concatenate([x_high, x_low], axis=0)
            ) + dot(low_ref[kind], x_high)
            parts.append(split(moved))
        return parts

    def sandwiched(atom, parts):
        rows = []
        for high, low in parts:
            for part in range(2):
                lanes = slice(LANES * part, LANES * (part + 1))
                pieces = []
                for mode in range(MODES):
                    points = slice(POINTS * mode, POINTS * (mode + 1))
                    pieces += [high[points, lanes], low[points, lanes]]
                rows.append(jnp.concatenate(pieces, axis=1))
        weights = []
        for mode in range(MODES):
            both = jnp.concatenate([weight_ref[MODES * atom + mode], blank], axis=0)
            weights += [
                both,
                jnp.concatenate([both[:, :LANES], jnp.zeros_like(both[:, LANES:])], axis=1),
            ]
        result = dot(jnp.concatenate(rows, axis=0), jnp.concatenate(weights, axis=0))
        return result[:, :LANES] + result[:, LANES:]

    rest_out = jnp.zeros((POINTS, LANES), jnp.float32)
    parts = shifted(0)
    for atom in range(ATOMS_HERE):
        following = shifted(atom + 1) if atom + 1 < ATOMS_HERE else None
        result = sandwiched(atom, parts)
        turned = [turn(result[POINTS * b : POINTS * (b + 1)], -28 * b) for b in range(4)]
        for t in range(3):
            out_ref[pl.ds(8 * t + atom, POINTS, stride=ROWS), :] = jnp.where(
                lane < PAIRS - 28 * t, turned[t], turned[t + 1]
            )
        rest_out = rest_out + turn(jnp.where(lane < 16, turned[3], 0.0), 16 * atom)
        parts = following
    out_ref[pl.ds(24, POINTS, stride=ROWS), :] = rest_out


def constants():
    pair = np.arange(LANES)
    valid = pair < PAIRS
    cols = np.zeros((LANES, 2 * LANES), np.float32)
    rows = np.zeros((2 * LANES, 16), np.float32)
    for k in range(ORB):
        cols[k, :LANES] = valid & (pair // ORB == k)
        cols[k, LANES:] = valid & (pair % ORB == k)
        rows[:LANES, k] = valid & (pair // ORB == k)
        rows[LANES:, k] = valid & (pair % ORB == k)
    return jnp.asarray(cols), jnp.asarray(rows)


def exchange(message, order):
    moved = lax.all_to_all(
        message.reshape(POINTS, ROWS, 1, LANES),
        AXES,
        split_axis=0,
        concat_axis=0,
        tiled=True,
        axis_index_groups=[order],
    )
    return moved.reshape(POINTS * ROWS, LANES)


def mixing(branch_weight, pair_branch):
    onehot = (
        pair_branch[:, :, None] == jnp.arange(branch_weight.shape[0], dtype=jnp.int32)
    ).astype(jnp.float32)
    return jnp.einsum("kjq,qm->mkj", onehot, branch_weight, precision=HIGHEST)


def on_device(
    out_order, back_order, green_blocks, couple_matrix, occupation, energy_shift, branch_weight, pair_branch
):
    f32, bf16 = jnp.float32, jnp.bfloat16
    out_spots = [out_order.index(device) for device in range(POINTS)]
    back_spots = [back_order.index(device) for device in range(POINTS)]
    smem = pl.BlockSpec(memory_space=pltpu.SMEM)
    vmem = pl.BlockSpec(memory_space=pltpu.VMEM)
    hbm = pl.BlockSpec(memory_space=pltpu.HBM)
    tiles = green_blocks.shape[4] // LANES
    message = pl.pallas_call(
        functools.partial(pack_kernel, out_spots),
        in_specs=[hbm],
        out_specs=hbm,
        out_shape=pltpu.HBM((POINTS * ROWS, LANES), f32),
        scratch_shapes=[
            pltpu.VMEM((400, tiles * LANES), f32),
            pltpu.VMEM((POINTS * ROWS, LANES), f32),
            pltpu.VMEM((LANES, LANES), f32),
            pltpu.SemaphoreType.DMA((3,)),
            pltpu.SemaphoreType.DMA((8,)),
        ],
        compiler_params=PARAMS,
        name="pack",
    )(constrain(green_blocks.reshape(400, tiles * LANES), pltpu.HBM))
    received = exchange(message, out_order)

    moments = pair_branch.shape[0]
    picks, energies = [], []
    for order in (back_order, out_order):
        pick = np.zeros((POINTS, moments), np.float32)
        pick[np.arange(POINTS), [place % moments for place in order]] = 1.0
        picks.append(pick)
        energies.append(jnp.asarray([place // moments for place in order], jnp.int32))
    table = mixing(branch_weight, pair_branch) / moments
    turned = couple_matrix.reshape(MODES, ORB, ORB, ATOMS_HERE).transpose(3, 0, 2, 1)
    turned = jnp.pad(turned, ((0, 0), (0, 0), (0, 6), (0, LANES - ORB))).reshape(-1, LANES)
    cols, rows = constants()
    weight, high, low = pl.pallas_call(
        prepare_kernel,
        in_specs=[smem, smem] + [vmem] * 8,
        out_specs=[vmem, vmem, vmem],
        out_shape=[
            pltpu.VMEM((ATOMS_HERE * MODES, DEPTH, 2 * LANES), bf16),
            pltpu.VMEM((2, MODES * POINTS, POINTS), bf16),
            pltpu.VMEM((2, MODES * POINTS, POINTS), bf16),
        ],
        compiler_params=PARAMS,
        cost_estimate=pl.CostEstimate(flops=10**9, bytes_accessed=4 * 10**6, transcendentals=0),
        name="prepare",
    )(
        occupation,
        energy_shift,
        turned,
        jnp.pad(table, ((0, 0), (0, 0), (0, LANES - moments))),
        cols,
        rows,
        jnp.asarray(np.pad(picks[0], ((0, 0), (0, LANES - moments)))),
        jnp.asarray(np.pad(picks[1].T, ((0, LANES - moments), (0, 0)))),
        energies[0][:, None],
        energies[1][None, :],
    )

    result = pl.pallas_call(
        compute_kernel,
        in_specs=[vmem] * 4,
        out_specs=vmem,
        out_shape=pltpu.VMEM((POINTS * ROWS, LANES), f32),
        compiler_params=PARAMS,
        name="compute",
    )(*(constrain(value, pltpu.VMEM) for value in (received, weight, high, low)))
    returned = exchange(result, back_order)
    out = pl.pallas_call(
        functools.partial(unpack_kernel, back_spots),
        in_specs=[vmem],
        out_specs=hbm,
        out_shape=pltpu.HBM((400, tiles * LANES), f32),
        scratch_shapes=[
            pltpu.VMEM((400, tiles * LANES), f32),
            pltpu.VMEM((LANES, LANES), f32),
            pltpu.SemaphoreType.DMA((9,)),
        ],
        compiler_params=PARAMS,
        name="unpack",
    )(constrain(returned, pltpu.VMEM))
    return out.reshape(green_blocks.shape)


def places(mesh, y_first):
    def key(place):
        energy, momentum = divmod(place, 8)
        x, y, z = momentum % 4, energy // 4, 2 * (momentum // 4) + (energy // 2) % 2
        return (energy % 2,) + ((y, z, x) if y_first else (x, y, z))

    return sorted(range(mesh.size), key=key)


def solution(mesh):
    in_specs = (
        P(None, "energy", "momentum", None, None),
        P(None, None, ("energy", "momentum")),
        P(),
        P(),
        P(),
        P(),
    )
    out_specs = P(None, "energy", "momentum", None, None)
    orders = places(mesh, True), places(mesh, False)
    return jax.shard_map(
        functools.partial(on_device, *orders), mesh=mesh, in_specs=in_specs, out_specs=out_specs, check_vma=False
    )
```
